512 devices in a mesh: replica: 64 (over x, y, core), section: 8 (over z).
Axes of the slice: x: 4, y: 8, z: 8, core: 2. Of those that a mesh axis runs over, the one named last changes fastest.
Arguments:
- gradients: bfloat16 [64, 512, 5120], P('replica', 'section')
- momentum: float32 [64, 512, 5120], P('replica', 'section'), may hold values from -12 to 12
- keep_block: int32 [64, 8, 80], P('replica', 'section'), may hold values from 0 to 63
Outputs:
- new_momentum: float32 [64, 512, 5120], P('replica', 'section')
- update: bfloat16 [512, 5120], P('section')
The draws below stay inside these ranges and needn't reach their ends.
All inputs are finite; a program needn't handle non-finite values.
Results may differ from the reference program's by a relative error of at most 0.0028.
Values may be sent and summed in bfloat16 or wider, within the bound.
A program may use at most 128 MiB of HBM per device.

```python
import jax
import jax.numpy as jnp
from jax import lax

D = 5120
GROUP = 64
BLOCK = 8
ROWS = 512
N_REPLICA = 64


def draw_gradients(key, part):
    key = jax.random.fold_in(key, 11)
    key_base, key_rows, key_cols = jax.random.split(key, 3)
    row_scale = jnp.exp(jax.random.uniform(key_rows, (1, ROWS, 1), jnp.float32, jnp.log(0.3), jnp.log(3.0)))
    col_scale = jnp.exp(jax.random.uniform(key_cols, (1, 1, D), jnp.float32, jnp.log(0.3), jnp.log(3.0)))
    rising = 3.0 ** (jnp.arange(ROWS, dtype=jnp.float32) / (ROWS - 1.0))
    base = jax.random.normal(key_base, (N_REPLICA, ROWS, D), jnp.float32)
    return (base * row_scale * col_scale * rising[None, :, None]).astype(jnp.bfloat16)


def plant(result, stream_key, low, largest):
    longest = result.shape.index(max(result.shape))
    spots = []
    for shift in (0, 1):
        where = [jax.random.randint(jax.random.fold_in(stream_key, axis), (), 0, length) for axis, length in enumerate(result.shape)]
        where[longest] = (where[longest] + shift) % result.shape[longest]
        spots.append(tuple(where))
    return result.at[spots[0]].set(low).at[spots[1]].set(largest)


def block_scale(stream_key, extent, cuts, smallest, top_value):
    def one(dim, shards_of):
        heights = jax.random.uniform(jax.random.fold_in(jax.random.fold_in(stream_key, 6), dim), (shards_of,), jnp.float32, smallest / len(cuts), top_value / len(cuts))
        return jnp.repeat(jnp.exp(heights), extent[dim] // shards_of).reshape((-1,) + (1,) * (len(extent) - dim - 1))

    gain = one(*cuts[0])
    for cut in cuts[1:]:
        gain = gain * one(*cut)
    return gain


def gaussian(stream_key, extent, spread, bound, pieces=(), kind=jnp.bfloat16):
    level = block_scale(stream_key, extent, pieces, -0.22, 0.18) if pieces else 1.0
    entries = jax.random.normal(stream_key, extent, jnp.float32) * spread * level
    return jnp.minimum(jnp.maximum(entries, -bound), bound).astype(kind)


def setup_inputs(seed: int = 0) -> dict:
    arg_keys = jax.random.split(jax.random.key(seed), 4)
    return {
        "gradients": draw_gradients(jax.random.fold_in(arg_keys[3], 71), 0),
        "momentum": gaussian(arg_keys[1], (N_REPLICA, ROWS, D), 2.0, 12.0, ((0, 64), (1, 8)), jnp.float32),
        "keep_block": plant(jax.random.randint(arg_keys[2], (N_REPLICA, ROWS // GROUP, D // GROUP), 0, (GROUP // BLOCK) ** 2), jax.random.fold_in(arg_keys[2], 1), 0, ((GROUP // BLOCK) ** 2) - 1).astype(jnp.int32),
    }


momentum_decay = 0.9
epsilon = 1e-06

def dct_basis():
    freq_index = jnp.arange(GROUP, dtype=jnp.float32)[:, None]
    cell_index = jnp.arange(GROUP, dtype=jnp.float32)[None, :]
    table = jnp.sqrt(2.0 / GROUP) * jnp.cos(jnp.pi * (2.0 * cell_index + 1.0) * freq_index / (2.0 * GROUP))
    first_row = jnp.where(jnp.arange(GROUP) == 0, 1.0 / jnp.sqrt(2.0), 1.0)
    return (table * first_row[:, None]).astype(jnp.float32)

def reference(gradients, momentum, keep_block):
    basis = dct_basis()
    row_blocks = ROWS // GROUP
    col_blocks = D // GROUP
    per_side = GROUP // BLOCK
    high = lax.Precision.HIGHEST

    def per_replica(carry, inputs):
        grad_slab, mom_slab, block_ids = inputs
        moments = momentum_decay * mom_slab + grad_slab.astype(jnp.float32)
        tile_grid = moments.reshape(row_blocks, GROUP, col_blocks, GROUP)
        spectrum = jnp.einsum('ki,ricj,lj->rkcl', basis, tile_grid, basis, precision=high)
        spectrum = spectrum.reshape(row_blocks, per_side, BLOCK, col_blocks, per_side, BLOCK)
        selector = (block_ids[..., None] == jnp.arange(per_side * per_side, dtype=jnp.int32)).astype(jnp.float32)
        selector = selector.reshape(row_blocks, col_blocks, per_side, per_side)
        kept_vals = jnp.einsum('rcyx,ryicxj->rcij', selector, spectrum, precision=high)
        own_dense = jnp.einsum('rcyx,rcij->ryicxj', selector, kept_vals, precision=high)
        own_space = jnp.einsum('ki,rkcl,lj->ricj', basis, own_dense.reshape(row_blocks, GROUP, col_blocks, GROUP), basis, precision=high)
        return (carry + own_dense, moments - own_space.reshape(ROWS, D))
    start = jnp.zeros((row_blocks, per_side, BLOCK, col_blocks, per_side, BLOCK), jnp.float32)
    dense_total, new_momentum = lax.scan(per_replica, start, (gradients, momentum, keep_block))
    total = jnp.einsum('ki,rkcl,lj->ricj', basis, dense_total.reshape(row_blocks, GROUP, col_blocks, GROUP), basis, precision=high)
    total = total.reshape(ROWS, D)
    scale = lax.rsqrt(jnp.mean(total * total) + epsilon)
    update = (total * scale).astype(jnp.bfloat16)
    return (new_momentum, update)
```

```python
import functools

import jax
import jax.numpy as jnp
import ml_dtypes
import numpy as np
from jax import lax
from jax.experimental import pallas as pl
from jax.experimental.pallas import tpu as pltpu
from jax.sharding import PartitionSpec as P

GROUP = 64
BLOCK = 8
SIDE = GROUP // BLOCK
LANES = 128
CHIPS_X, CHIPS_Y, CORES = 4, 8, 2
OWNERS = CHIPS_X * CORES
MESH = pl.DeviceIdType.MESH
F32, BF16 = jnp.float32, jnp.bfloat16

momentum_decay = 0.9
epsilon = 1e-06


def dct_basis():
    k = np.arange(GROUP, dtype=np.float64)[:, None]
    n = np.arange(GROUP, dtype=np.float64)[None, :]
    basis = np.sqrt(2.0 / GROUP) * np.cos(np.pi * (2.0 * n + 1.0) * k / (2.0 * GROUP))
    basis[0] /= np.sqrt(2.0)
    return basis.astype(np.float32)


def two_terms(values):
    high = values.astype(ml_dtypes.bfloat16)
    low = (values - high.astype(np.float32)).astype(ml_dtypes.bfloat16)
    return high, low


def constant_tables():
    basis = dct_basis()

    def right(matrix):
        high, low = two_terms(np.kron(np.eye(2, dtype=np.float32), matrix))
        return np.concatenate([high, high, low], axis=0)

    def left(matrix):
        high, low = two_terms(matrix)
        wide = np.concatenate([high, high, low, np.zeros_like(low)], axis=1)
        return np.concatenate([wide[:, :LANES], wide[:, LANES:]], axis=0)

    return np.concatenate([right(basis.T), right(basis), left(basis), left(basis.T)], axis=0)


def split(values):
    high = values.astype(BF16)
    low = (values - high.astype(F32)).astype(BF16)
    return high, low


def mm(a, b):
    return jnp.dot(a, b, preferred_element_type=F32)


def kernel(
    entry_count, pairs, kb_ref, g_ref, m_ref, tab_ref, nm_ref, upd_ref,
    g_buf, x_buf, tab, masked, fold, spread, compact, tiles_x, tiles_y, sums_x, sums_z, upd,
    g_sem, m_sem, tab_sem, nm_sem, out_sem,
    x_send, x_recv, y_send, y_recv, sx_send, sx_recv, sz_send, sz_recv, f_send, f_recv, c_send, c_recv,
):
    width = pairs * LANES
    n_blocks = 2 * pairs
    replica, section = lax.axis_index("replica"), lax.axis_index("section")
    x = replica // (CHIPS_Y * CORES)
    y = (replica // CORES) % CHIPS_Y
    core = replica % CORES
    mine = x * CORES + core

    def peer(dx=0, dy=0, dc=0, dz=0):
        px, py, pc = (x + dx) % CHIPS_X, (y + dy) % CHIPS_Y, (core + dc) % CORES
        return ((px * CHIPS_Y + py) * CORES + pc, (section + dz) % 8)

    group_x = [(dx, dc) for dx in range(CHIPS_X) for dc in range(CORES)][1:]

    loads = []
    tab_load = pltpu.make_async_copy(tab_ref, tab, tab_sem)
    for s in range(OWNERS):
        cols = slice(s * width, (s + 1) * width)
        pair = (
            pltpu.make_async_copy(m_ref.at[:, cols], x_buf.at[:, cols], m_sem.at[s]),
            pltpu.make_async_copy(g_ref.at[:, cols], g_buf.at[:, cols], g_sem.at[s]),
        )
        loads.append(pair)
        pair[0].start()
        pair[1].start()
        if s == 0:
            tab_load.start()

    barrier = pltpu.get_barrier_semaphore()
    everyone = (
        [peer(dx=dx, dc=dc) for dx, dc in group_x]
        + [peer(dy=d) for d in range(1, CHIPS_Y)]
        + [peer(dz=d) for d in range(1, 8)]
    )
    for other in everyone:
        pl.semaphore_signal(barrier, inc=1, device_id=other, device_id_type=MESH)

    lane8 = lax.broadcasted_iota(jnp.int32, (BLOCK, LANES), 1)
    upper = lane8 >= GROUP
    lane_q = (lane8 % GROUP) // BLOCK
    row_f = lax.broadcasted_iota(jnp.int32, (width, LANES), 0)
    lane_f = lax.broadcasted_iota(jnp.int32, (width, LANES), 1)
    fold[...] = jnp.where((row_f // GROUP) * BLOCK + row_f % BLOCK == lane_f, 1.0, 0.0).astype(BF16)
    row_t = lax.broadcasted_iota(jnp.int32, (LANES, width), 0)
    lane_t = lax.broadcasted_iota(jnp.int32, (LANES, width), 1)
    block_t = lane_t // GROUP
    spread[:, 0:width] = jnp.where(row_t == block_t * BLOCK + lane_t % BLOCK, 1.0, 0.0).astype(BF16)
    spread[:, width : 2 * width] = jnp.where(row_t == BLOCK * n_blocks + block_t, 1.0, 0.0).astype(BF16)
    spread[:, 2 * width : 3 * width] = jnp.where(row_t == (BLOCK + 1) * n_blocks + block_t, 1.0, 0.0).astype(BF16)

    tab_load.wait()
    right_fwd = tab[0:384, :]
    right_inv = tab[384:768, :]
    left_fwd = jnp.concatenate([tab[768:832, :], tab[832:896, 0:64]], axis=1)
    left_inv = jnp.concatenate([tab[896:960, :], tab[960:1024, 0:64]], axis=1)

    def block_rows(s, j):
        c = s * n_blocks + 2 * j
        return kb_ref[0, c], kb_ref[0, c + 1]

    def p_lanes(s, j):
        k0, k1 = block_rows(s, j)
        return jnp.where(upper, k1 // SIDE, k0 // SIDE)

    def q_lanes(s, j):
        k0, k1 = block_rows(s, j)
        return jnp.where(upper, k1 % SIDE, k0 % SIDE)

    for s in range(OWNERS):
        cols = slice(s * width, (s + 1) * width)
        loads[s][0].wait()
        loads[s][1].wait()
        moments = momentum_decay * x_buf[:, cols] + g_buf[:, cols].astype(F32)
        x_buf[:, cols] = moments
        high, low = split(moments)
        rows = mm(left_fwd, jnp.concatenate([high, low, high], axis=0))
        chosen = []
        for j in range(pairs):
            p_of = p_lanes(s, j)
            picked = jnp.zeros((BLOCK, LANES), F32)
            for p in range(SIDE):
                picked = jnp.where(p_of == p, rows[p * BLOCK : (p + 1) * BLOCK, j * LANES : (j + 1) * LANES], picked)
            chosen.append(picked)
        high, low = split(jnp.concatenate(chosen, axis=0))
        spectrum = mm(jnp.concatenate([high, low, high], axis=1), right_fwd)
        for j in range(pairs):
            kept = jnp.where(q_lanes(s, j) == lane_q, spectrum[j * BLOCK : (j + 1) * BLOCK, :], 0.0)
            masked[s * BLOCK : (s + 1) * BLOCK, j * LANES : (j + 1) * LANES] = kept

    high, low = split(masked[...])
    packed = mm(high, fold[...]) + mm(low, fold[...])
    for s in range(OWNERS):
        tile = packed[s * BLOCK : (s + 1) * BLOCK, :]
        for b in range(n_blocks):
            k = kb_ref[0, s * n_blocks + b]
            tile = jnp.where(lane8 == BLOCK * n_blocks + b, (k // SIDE).astype(F32), tile)
            tile = jnp.where(lane8 == (BLOCK + 1) * n_blocks + b, (k % SIDE).astype(F32), tile)
        compact[s] = tile

    pl.semaphore_wait(barrier, len(everyone))

    sends_x = []
    for i, (dx, dc) in enumerate(group_x, start=1):
        px, pc = (x + dx) % CHIPS_X, (core + dc) % CORES
        copy = pltpu.make_async_remote_copy(
            src_ref=compact.at[px * CORES + pc], dst_ref=tiles_x.at[i], send_sem=x_send.at[i], recv_sem=x_recv.at[i],
            device_id=peer(dx=dx, dc=dc), device_id_type=MESH,
        )
        copy.start()
        sends_x.append(copy)
    tiles_x[0] = compact[mine]

    stores = []

    def own_part(s):
        cols = slice(s * width, (s + 1) * width)
        stacked = jnp.concatenate(
            [masked[s * BLOCK : (s + 1) * BLOCK, j * LANES : (j + 1) * LANES] for j in range(pairs)], axis=0
        )
        high, low = split(stacked)
        wide = mm(jnp.concatenate([high, low, high], axis=1), right_inv)
        placed = []
        for j in range(pairs):
            p_of = p_lanes(s, j)
            piece = wide[j * BLOCK : (j + 1) * BLOCK, :]
            placed.append(jnp.concatenate([jnp.where(p_of == p, piece, 0.0) for p in range(SIDE)], axis=0))
        high, low = split(jnp.concatenate(placed, axis=1))
        own = mm(left_inv, jnp.concatenate([high, low, high], axis=0))
        x_buf[:, cols] = x_buf[:, cols] - own
        copy = pltpu.make_async_copy(x_buf.at[:, cols], nm_ref.at[:, cols], nm_sem.at[s])
        copy.start()
        stores.append(copy)

    for s in range(0, 3):
        own_part(s)

    for copy in sends_x:
        copy.wait_recv()

    tiles_y[0] = tiles_x[...]
    sends_y = []
    for d in range(1, CHIPS_Y):
        copy = pltpu.make_async_remote_copy(
            src_ref=tiles_x, dst_ref=tiles_y.at[d], send_sem=y_send.at[d], recv_sem=y_recv.at[d],
            device_id=peer(dy=d), device_id_type=MESH,
        )
        copy.start()
        sends_y.append(copy)

    for s in range(3, OWNERS):
        own_part(s)

    for copy in sends_y:
        copy.wait_recv()

    n_rows = CHIPS_Y * OWNERS * BLOCK
    received = tiles_y[...].reshape(n_rows, LANES)
    high, low = split(received)
    lane_r = lax.broadcasted_iota(jnp.int32, (n_rows, LANES), 1) % GROUP
    row_r = lax.broadcasted_iota(jnp.int32, (n_rows, LANES), 0) % BLOCK
    group_r = (lane_r // BLOCK).astype(F32)
    same_row = (lane_r % BLOCK) == row_r
    total_spectrum = []
    for j in range(pairs):
        part = slice(j * LANES, (j + 1) * LANES)
        values = mm(high, spread[:, part]) + mm(low, spread[:, part])
        p_of = mm(high, spread[:, width + j * LANES : width + (j + 1) * LANES])
        q_of = mm(high, spread[:, 2 * width + j * LANES : 2 * width + (j + 1) * LANES])
        values = jnp.where(q_of == group_r, values, 0.0)
        place = jnp.where(same_row & (p_of == group_r), 1.0, 0.0).astype(BF16)
        v_high, v_low = split(values)
        dims = (((0,), (0,)), ((), ()))
        both = lax.dot_general(place, v_high, dims, preferred_element_type=F32) + lax.dot_general(
            place, v_low, dims, preferred_element_type=F32
        )
        lane64 = lax.broadcasted_iota(jnp.int32, (GROUP, LANES), 1)
        total_spectrum.append(jnp.where(lane64 >= GROUP, both[GROUP:, :], both[:GROUP, :]))

    squares = jnp.zeros((BLOCK, LANES), F32)
    for part in total_spectrum:
        for p in range(SIDE):
            piece = part[p * BLOCK : (p + 1) * BLOCK, :]
            squares = squares + piece * piece
    sums_x[0] = squares
    sends_sx = []
    for i, (dx, dc) in enumerate(group_x, start=1):
        copy = pltpu.make_async_remote_copy(
            src_ref=sums_x.at[0], dst_ref=sums_x.at[i], send_sem=sx_send.at[i], recv_sem=sx_recv.at[i],
            device_id=peer(dx=dx, dc=dc), device_id_type=MESH,
        )
        copy.start()
        sends_sx.append(copy)

    high, low = split(jnp.concatenate(total_spectrum, axis=0))
    wide = mm(jnp.concatenate([high, low, high], axis=1), right_inv)
    high, low = split(jnp.concatenate([wide[j * GROUP : (j + 1) * GROUP, :] for j in range(pairs)], axis=1))
    total = mm(left_inv, jnp.concatenate([high, low, high], axis=0))

    for copy in sends_sx:
        copy.wait_recv()
    sums_z[0] = jnp.sum(sums_x[...], axis=0)
    sends_sz = []
    for d in range(1, 8):
        copy = pltpu.make_async_remote_copy(
            src_ref=sums_z.at[0], dst_ref=sums_z.at[d], send_sem=sz_send.at[d], recv_sem=sz_recv.at[d],
            device_id=peer(dz=d), device_id_type=MESH,
        )
        copy.start()
        sends_sz.append(copy)
    for copy in sends_sz:
        copy.wait_recv()
    everything = jnp.sum(sums_z[...], axis=0)
    square_sum = jnp.sum(jnp.sum(everything, axis=0, keepdims=True), axis=1, keepdims=True)
    scale = lax.rsqrt(square_sum / entry_count + epsilon)
    upd[mine] = (total * scale).astype(BF16)

    def to_core(slot, i):
        return pltpu.make_async_remote_copy(
            src_ref=upd.at[slot], dst_ref=upd.at[slot], send_sem=c_send.at[i], recv_sem=c_recv.at[i],
            device_id=peer(dc=1), device_id_type=MESH,
        )

    def to_out(slot, i):
        return pltpu.make_async_copy(
            upd.at[slot], upd_ref.at[:, pl.ds(pl.multiple_of(slot * width, LANES), width)], out_sem.at[i]
        )

    sends_f, sends_c, outs = [], [], []
    for d in (1, 3, 2):
        copy = pltpu.make_async_remote_copy(
            src_ref=upd.at[mine], dst_ref=upd.at[mine], send_sem=f_send.at[d], recv_sem=f_recv.at[d],
            device_id=peer(dx=d), device_id_type=MESH,
        )
        copy.start()
        sends_f.append(copy)
    copy = to_core(mine, 0)
    copy.start()
    sends_c.append(copy)
    copy = to_out(mine, 0)
    copy.start()
    outs.append(copy)
    for d in (1, 3, 2):
        slot = ((x + CHIPS_X - d) % CHIPS_X) * CORES + core
        pltpu.make_async_remote_copy(
            src_ref=upd.at[slot], dst_ref=upd.at[slot], send_sem=f_send.at[d], recv_sem=f_recv.at[d],
            device_id=peer(dx=d), device_id_type=MESH,
        ).wait_recv()
        copy = to_core(slot, d)
        copy.start()
        sends_c.append(copy)
        copy = to_out(slot, d)
        copy.start()
        outs.append(copy)
    for i, d in enumerate((0, 1, 3, 2)):
        slot = ((x + CHIPS_X - d) % CHIPS_X) * CORES + (core + 1) % CORES
        pltpu.make_async_remote_copy(
            src_ref=upd.at[slot], dst_ref=upd.at[slot], send_sem=c_send.at[d], recv_sem=c_recv.at[d],
            device_id=peer(dc=1), device_id_type=MESH,
        ).wait_recv()
        copy = to_out(slot, 4 + i)
        copy.start()
        outs.append(copy)

    for copy in sends_x + sends_y + sends_sx + sends_sz + sends_f + sends_c:
        copy.wait_send()
    for copy in stores + outs:
        copy.wait()


def per_device(gradients, momentum, keep_block):
    local_rows, columns = gradients.shape[1:]
    pairs = columns // (OWNERS * LANES)
    width = pairs * LANES
    tables = jnp.asarray(constant_tables())
    entry_count = float(local_rows * lax.axis_size("section") * columns)
    dma = pltpu.SemaphoreType.DMA
    new_momentum, update = pl.pallas_call(
        functools.partial(kernel, entry_count, pairs),
        out_shape=(
            jax.ShapeDtypeStruct((local_rows, columns), F32),
            jax.ShapeDtypeStruct((local_rows, columns), BF16),
        ),
        in_specs=[pl.BlockSpec(memory_space=pltpu.SMEM)] + [pl.BlockSpec(memory_space=pl.ANY)] * 3,
        out_specs=(pl.BlockSpec(memory_space=pl.ANY), pl.BlockSpec(memory_space=pl.ANY)),
        scratch_shapes=[
            pltpu.VMEM((local_rows, columns), BF16),
            pltpu.VMEM((local_rows, columns), F32),
            pltpu.VMEM(tables.shape, BF16),
            pltpu.VMEM((OWNERS * BLOCK, width), F32),
            pltpu.VMEM((width, LANES), BF16),
            pltpu.VMEM((LANES, 3 * width), BF16),
            pltpu.VMEM((OWNERS, BLOCK, LANES), F32),
            pltpu.VMEM((OWNERS, BLOCK, LANES), F32),
            pltpu.VMEM((CHIPS_Y, OWNERS, BLOCK, LANES), F32),
            pltpu.VMEM((OWNERS, BLOCK, LANES), F32),
            pltpu.VMEM((8, BLOCK, LANES), F32),
            pltpu.VMEM((OWNERS, local_rows, width), BF16),
            dma((OWNERS,)), dma((OWNERS,)), dma, dma((OWNERS,)), dma((OWNERS,)),
            dma((OWNERS,)), dma((OWNERS,)), dma((CHIPS_Y,)), dma((CHIPS_Y,)),
            dma((OWNERS,)), dma((OWNERS,)), dma((8,)), dma((8,)),
            dma((CHIPS_X,)), dma((CHIPS_X,)), dma((CHIPS_X,)), dma((CHIPS_X,)),
        ],
        compiler_params=pltpu.CompilerParams(collective_id=0, has_side_effects=True, vmem_limit_bytes=60 << 20),
        name="kept_blocks_step",
    )(keep_block[0], gradients[0], momentum[0], tables)
    return new_momentum[None], update


def solution(mesh):
    placed = (
        P("replica", "section", None),
        P("replica", "section", None),
        P("replica", "section", None),
    )
    return jax.shard_map(
        per_device,
        mesh=mesh,
        in_specs=placed,
        out_specs=(P("replica", "section", None), P("section", None)),
        check_vma=False,
    )
```

```python
import functools

import jax
import jax.numpy as jnp
import ml_dtypes
import numpy as np
from jax import lax
from jax.experimental import pallas as pl
from jax.experimental.pallas import tpu as pltpu
from jax.sharding import PartitionSpec as P

GROUP = 64
BLOCK = 8
SIDE = GROUP // BLOCK
LANES = 128
CHIPS_X, CHIPS_Y, CORES, SECTIONS = 4, 8, 2, 8
OWNERS = CHIPS_X * CORES
MESH = pl.DeviceIdType.MESH
F32, BF16 = jnp.float32, jnp.bfloat16

momentum_decay = 0.9
epsilon = 1e-06


def dct_basis():
    k = np.arange(GROUP, dtype=np.float64)[:, None]
    n = np.arange(GROUP, dtype=np.float64)[None, :]
    basis = np.sqrt(2.0 / GROUP) * np.cos(np.pi * (2.0 * n + 1.0) * k / (2.0 * GROUP))
    basis[0] /= np.sqrt(2.0)
    return basis.astype(np.float32)


def two_terms(values):
    high = values.astype(ml_dtypes.bfloat16)
    low = (values - high.astype(np.float32)).astype(ml_dtypes.bfloat16)
    return high, low


def constant_tables():
    basis = dct_basis()

    def right(matrix):
        high, low = two_terms(np.kron(np.eye(2, dtype=np.float32), matrix))
        return np.concatenate([high, high, low], axis=0)

    def left(matrix):
        high, low = two_terms(matrix)
        wide = np.concatenate([high, high, low, np.zeros_like(low)], axis=1)
        return np.concatenate([wide[:, :LANES], wide[:, LANES:]], axis=0)

    return np.concatenate([right(basis.T), right(basis), left(basis), left(basis.T)], axis=0)


def split(values):
    high = values.astype(BF16)
    low = (values - high.astype(F32)).astype(BF16)
    return high, low


def mm(a, b):
    return jnp.dot(a, b, preferred_element_type=F32)


def kernel(
    pairs, kb_hbm, g_ref, m_ref, tab_ref, nm_ref, total_ref, sums_ref,
    kb_ref, g_buf, m_buf, tab, masked, fold, spread, compact, tiles_x, tiles_y, sums_x,
    load_sem, kb_sem, send_sem, recv_sem, gather_send, gather_recv,
):
    width = pairs * LANES
    n_blocks = 2 * pairs
    replica, section = lax.axis_index("replica"), lax.axis_index("section")
    x = replica // (CHIPS_Y * CORES)
    y = (replica // CORES) % CHIPS_Y
    core = replica % CORES
    mine = x * CORES + core

    def peer(dx=0, dy=0, dc=0, dz=0):
        px, py, pc = (x + dx) % CHIPS_X, (y + dy) % CHIPS_Y, (core + dc) % CORES
        return ((px * CHIPS_Y + py) * CORES + pc, (section + dz) % SECTIONS)

    group_x = [(dx, dc) for dx in range(CHIPS_X) for dc in range(CORES)][1:]

    half = OWNERS // 2 * width
    loads = []
    kb_load = pltpu.make_async_copy(kb_hbm, kb_ref, kb_sem)
    tab_load = pltpu.make_async_copy(tab_ref, tab, load_sem.at[4])
    for h in range(2):
        cols = slice(h * half, (h + 1) * half)
        pair = (
            pltpu.make_async_copy(m_ref.at[:, cols], m_buf.at[:, cols], load_sem.at[2 * h]),
            pltpu.make_async_copy(g_ref.at[:, cols], g_buf.at[:, cols], load_sem.at[2 * h + 1]),
        )
        loads.append(pair)
        pair[0].start()
        pair[1].start()
        if h == 0:
            kb_load.start()
            tab_load.start()

    barrier = pltpu.get_barrier_semaphore()
    everyone = (
        [peer(dx=dx, dc=dc) for dx, dc in group_x]
        + [peer(dy=d) for d in range(1, CHIPS_Y)]
        + [peer(dz=d) for d in range(1, SECTIONS)]
    )
    for other in everyone:
        pl.semaphore_signal(barrier, inc=1, device_id=other, device_id_type=MESH)

    lane8 = lax.broadcasted_iota(jnp.int32, (BLOCK, LANES), 1)
    upper = lane8 >= GROUP
    lane_q = (lane8 % GROUP) // BLOCK
    row_f = lax.broadcasted_iota(jnp.int32, (width, LANES), 0)
    lane_f = lax.broadcasted_iota(jnp.int32, (width, LANES), 1)
    fold[...] = jnp.where((row_f // GROUP) * BLOCK + row_f % BLOCK == lane_f, 1.0, 0.0).astype(BF16)
    row_t = lax.broadcasted_iota(jnp.int32, (LANES, width), 0)
    lane_t = lax.broadcasted_iota(jnp.int32, (LANES, width), 1)
    block_t = lane_t // GROUP
    spread[:, 0:width] = jnp.where(row_t == block_t * BLOCK + lane_t % BLOCK, 1.0, 0.0).astype(BF16)
    spread[:, width : 2 * width] = jnp.where(row_t == BLOCK * n_blocks + block_t, 1.0, 0.0).astype(BF16)
    spread[:, 2 * width : 3 * width] = jnp.where(row_t == (BLOCK + 1) * n_blocks + block_t, 1.0, 0.0).astype(BF16)

    kb_load.wait()
    tab_load.wait()
    right_fwd = tab[0:384, :]
    right_inv = tab[384:768, :]
    left_fwd = jnp.concatenate([tab[768:832, :], tab[832:896, 0:64]], axis=1)
    left_inv = jnp.concatenate([tab[896:960, :], tab[960:1024, 0:64]], axis=1)

    def block_pair(s, j):
        c = s * n_blocks + 2 * j
        return kb_ref[0, c], kb_ref[0, c + 1]

    def p_lanes(s, j):
        k0, k1 = block_pair(s, j)
        return jnp.where(upper, k1 // SIDE, k0 // SIDE)

    def q_lanes(s, j):
        k0, k1 = block_pair(s, j)
        return jnp.where(upper, k1 % SIDE, k0 % SIDE)

    chosen = []
    for s in range(OWNERS):
        if s % (OWNERS // 2) == 0:
            for copy in loads[s // (OWNERS // 2)]:
                copy.wait()
        cols = slice(s * width, (s + 1) * width)
        moments = momentum_decay * m_buf[:, cols] + g_buf[:, cols].astype(F32)
        nm_ref[:, cols] = moments
        high, low = split(moments)
        rows = mm(left_fwd, jnp.concatenate([high, low, high], axis=0))
        for j in range(pairs):
            p_of = p_lanes(s, j)
            picked = jnp.zeros((BLOCK, LANES), F32)
            for p in range(SIDE):
                picked = jnp.where(p_of == p, rows[p * BLOCK : (p + 1) * BLOCK, j * LANES : (j + 1) * LANES], picked)
            chosen.append(picked)

    high, low = split(jnp.concatenate(chosen, axis=0))
    spectrum = mm(jnp.concatenate([high, low, high], axis=1), right_fwd)
    for s in range(OWNERS):
        for j in range(pairs):
            row = (s * pairs + j) * BLOCK
            kept = jnp.where(q_lanes(s, j) == lane_q, spectrum[row : row + BLOCK, :], 0.0)
            masked[s * BLOCK : (s + 1) * BLOCK, j * LANES : (j + 1) * LANES] = kept

    high, low = split(masked[...])
    packed = mm(high, fold[...]) + mm(low, fold[...])
    for s in range(OWNERS):
        tile = packed[s * BLOCK : (s + 1) * BLOCK, :]
        for b in range(n_blocks):
            k = kb_ref[0, s * n_blocks + b]
            tile = jnp.where(lane8 == BLOCK * n_blocks + b, (k // SIDE).astype(F32), tile)
            tile = jnp.where(lane8 == (BLOCK + 1) * n_blocks + b, (k % SIDE).astype(F32), tile)
        compact[s] = tile

    pl.semaphore_wait(barrier, len(everyone))

    def send(src, dst, i, other):
        copy = pltpu.make_async_remote_copy(
            src_ref=src, dst_ref=dst, send_sem=send_sem.at[i], recv_sem=recv_sem.at[i],
            device_id=other, device_id_type=MESH,
        )
        copy.start()

    def all_of(ref, i):
        return pltpu.make_async_remote_copy(
            src_ref=ref, dst_ref=ref, send_sem=send_sem.at[i], recv_sem=recv_sem.at[i],
            device_id=peer(dc=1), device_id_type=MESH,
        )

    for i, (dx, dc) in enumerate(group_x, start=1):
        px, pc = (x + dx) % CHIPS_X, (core + dc) % CORES
        send(compact.at[px * CORES + pc], tiles_x.at[i], 0, peer(dx=dx, dc=dc))
    tiles_x[0] = compact[mine]

    wide = []
    for s in range(OWNERS):
        stacked = jnp.concatenate(
            [masked[s * BLOCK : (s + 1) * BLOCK, j * LANES : (j + 1) * LANES] for j in range(pairs)], axis=0
        )
        wide.append(stacked)
    high, low = split(jnp.concatenate(wide, axis=0))
    wide = mm(jnp.concatenate([high, low, high], axis=1), right_inv)
    for s in range(OWNERS):
        cols = slice(s * width, (s + 1) * width)
        placed = []
        for j in range(pairs):
            p_of = p_lanes(s, j)
            row = (s * pairs + j) * BLOCK
            piece = wide[row : row + BLOCK, :]
            placed.append(jnp.concatenate([jnp.where(p_of == p, piece, 0.0) for p in range(SIDE)], axis=0))
        high, low = split(jnp.concatenate(placed, axis=1))
        nm_ref[:, cols] = nm_ref[:, cols] - mm(left_inv, jnp.concatenate([high, low, high], axis=0))

    all_of(tiles_x.at[1:OWNERS], 0).wait_recv()

    tiles_y[0] = tiles_x[...]
    for d in range(1, CHIPS_Y):
        send(tiles_x, tiles_y.at[d], 1, peer(dy=d))
    all_of(tiles_y.at[1:CHIPS_Y], 1).wait_recv()

    n_rows = CHIPS_Y * OWNERS * BLOCK
    high, low = split(tiles_y[...].reshape(n_rows, LANES))
    lane_r = lax.broadcasted_iota(jnp.int32, (n_rows, LANES), 1) % GROUP
    row_r = lax.broadcasted_iota(jnp.int32, (n_rows, LANES), 0) % BLOCK
    group_r = (lane_r // BLOCK).astype(F32)
    same_row = (lane_r % BLOCK) == row_r
    lane64 = lax.broadcasted_iota(jnp.int32, (GROUP, LANES), 1)
    total_spectrum = []
    for j in range(pairs):
        part = slice(j * LANES, (j + 1) * LANES)
        values = mm(high, spread[:, part]) + mm(low, spread[:, part])
        p_of = mm(high, spread[:, width + j * LANES : width + (j + 1) * LANES])
        q_of = mm(high, spread[:, 2 * width + j * LANES : 2 * width + (j + 1) * LANES])
        values = jnp.where(q_of == group_r, values, 0.0)
        place = jnp.where(same_row & (p_of == group_r), 1.0, 0.0).astype(BF16)
        v_high, v_low = split(values)
        dims = (((0,), (0,)), ((), ()))
        both = lax.dot_general(place, v_high, dims, preferred_element_type=F32) + lax.dot_general(
            place, v_low, dims, preferred_element_type=F32
        )
        total_spectrum.append(jnp.where(lane64 >= GROUP, both[GROUP:, :], both[:GROUP, :]))

    squares = jnp.zeros((BLOCK, LANES), F32)
    for part in total_spectrum:
        for p in range(SIDE):
            piece = part[p * BLOCK : (p + 1) * BLOCK, :]
            squares = squares + piece * piece
    sums_x[0] = squares
    for i, (dx, dc) in enumerate(group_x, start=1):
        send(sums_x.at[0], sums_x.at[i], 2, peer(dx=dx, dc=dc))

    high, low = split(jnp.concatenate(total_spectrum, axis=0))
    wide = mm(jnp.concatenate([high, low, high], axis=1), right_inv)
    high, low = split(jnp.concatenate([wide[j * GROUP : (j + 1) * GROUP, :] for j in range(pairs)], axis=1))
    total_ref[mine] = mm(left_inv, jnp.concatenate([high, low, high], axis=0))

    def gather(slot, i, other):
        return pltpu.make_async_remote_copy(
            src_ref=total_ref.at[slot], dst_ref=total_ref.at[slot],
            send_sem=gather_send.at[i], recv_sem=gather_recv.at[i], device_id=other, device_id_type=MESH,
        )

    sends = [gather(mine, d, peer(dx=d)) for d in (1, 3, 2)] + [gather(mine, 4, peer(dc=1))]
    for copy in sends:
        copy.start()

    all_of(sums_x.at[1:OWNERS], 2).wait_recv()
    sums_ref[0] = jnp.sum(sums_x[...], axis=0)
    for d in range(1, SECTIONS):
        send(sums_ref.at[0], sums_ref.at[d], 3, peer(dz=d))

    for d in (1, 3, 2):
        slot = ((x + CHIPS_X - d) % CHIPS_X) * CORES + core
        gather(slot, d, peer(dx=d)).wait_recv()
        copy = gather(slot, 4 + d, peer(dc=1))
        copy.start()
        sends.append(copy)
    for d in (0, 1, 3, 2):
        slot = ((x + CHIPS_X - d) % CHIPS_X) * CORES + (core + 1) % CORES
        gather(slot, 4 + d, peer(dc=1)).wait_recv()

    all_of(sums_ref.at[1:SECTIONS], 3).wait_recv()
    all_of(compact.at[1:OWNERS], 0).wait_send()
    all_of(tiles_y.at[1:CHIPS_Y], 1).wait_send()
    all_of(sums_x.at[1:OWNERS], 2).wait_send()
    all_of(sums_ref.at[1:SECTIONS], 3).wait_send()
    for copy in sends:
        copy.wait_send()


def per_device(gradients, momentum, keep_block):
    local_rows, columns = gradients.shape[1:]
    pairs = columns // (OWNERS * LANES)
    width = pairs * LANES
    tables = jnp.asarray(constant_tables())
    entry_count = float(local_rows * lax.axis_size("section") * columns)
    dma = pltpu.SemaphoreType.DMA
    new_momentum, total, sums = pl.pallas_call(
        functools.partial(kernel, pairs),
        out_shape=(
            pltpu.VMEM((local_rows, columns), F32),
            pltpu.VMEM((OWNERS, local_rows, width), F32),
            pltpu.VMEM((SECTIONS, BLOCK, LANES), F32),
        ),
        in_specs=[pl.BlockSpec(memory_space=pltpu.HBM)] * 4,
        out_specs=(pl.BlockSpec(memory_space=pltpu.VMEM),) * 3,
        scratch_shapes=[
            pltpu.SMEM(keep_block.shape[1:], jnp.int32),
            pltpu.VMEM((local_rows, columns), BF16),
            pltpu.VMEM((local_rows, columns), F32),
            pltpu.VMEM(tables.shape, BF16),
            pltpu.VMEM((OWNERS * BLOCK, width), F32),
            pltpu.VMEM((width, LANES), BF16),
            pltpu.VMEM((LANES, 3 * width), BF16),
            pltpu.VMEM((OWNERS, BLOCK, LANES), F32),
            pltpu.VMEM((OWNERS, BLOCK, LANES), F32),
            pltpu.VMEM((CHIPS_Y, OWNERS, BLOCK, LANES), F32),
            pltpu.VMEM((OWNERS, BLOCK, LANES), F32),
            dma((5,)), dma, dma((4,)), dma((4,)), dma((OWNERS,)), dma((OWNERS,)),
        ],
        compiler_params=pltpu.CompilerParams(collective_id=0, has_side_effects=True, vmem_limit_bytes=56 << 20),
        name="kept_blocks_step",
    )(keep_block[0], gradients[0], momentum[0], tables)
    scale = lax.rsqrt(jnp.sum(sums) / entry_count + epsilon)
    update = (jnp.transpose(total, (1, 0, 2)).reshape(local_rows, columns) * scale).astype(BF16)
    return new_momentum[None], update


def solution(mesh):
    placed = (
        P("replica", "section", None),
        P("replica", "section", None),
        P("replica", "section", None),
    )
    return jax.shard_map(
        per_device,
        mesh=mesh,
        in_specs=placed,
        out_specs=(P("replica", "section", None), P("section", None)),
        check_vma=False,
    )
```

```python
import functools

import jax
import jax.numpy as jnp
import ml_dtypes
import numpy as np
from jax import lax
from jax.experimental import pallas as pl
from jax.experimental.pallas import tpu as pltpu
from jax.sharding import PartitionSpec as P

GROUP = 64
BLOCK = 8
SIDE = GROUP // BLOCK
LANES = 128
CHIPS_X, CHIPS_Y, CORES, SECTIONS = 4, 8, 2, 8
OWNERS = CHIPS_X * CORES
MESH = pl.DeviceIdType.MESH
F32, BF16 = jnp.float32, jnp.bfloat16

momentum_decay = 0.9
epsilon = 1e-06


def dct_basis():
    k = np.arange(GROUP, dtype=np.float64)[:, None]
    n = np.arange(GROUP, dtype=np.float64)[None, :]
    basis = np.sqrt(2.0 / GROUP) * np.cos(np.pi * (2.0 * n + 1.0) * k / (2.0 * GROUP))
    basis[0] /= np.sqrt(2.0)
    return basis.astype(np.float32)


def two_terms(values):
    high = values.astype(ml_dtypes.bfloat16)
    low = (values - high.astype(np.float32)).astype(ml_dtypes.bfloat16)
    return high, low


def constant_tables():
    basis = dct_basis()

    def right(matrix):
        high, low = two_terms(np.kron(np.eye(2, dtype=np.float32), matrix))
        return np.concatenate([high, high, low], axis=0)

    def left(matrix):
        high, low = two_terms(matrix)
        wide = np.concatenate([high, high, low, np.zeros_like(low)], axis=1)
        return np.concatenate([wide[:, :LANES], wide[:, LANES:]], axis=0)

    by_row_in_block = np.arange(GROUP).reshape(SIDE, BLOCK).T.reshape(-1)
    return np.concatenate(
        [right(basis.T), right(basis), left(basis), left(basis.T), left(basis.T[:, by_row_in_block])], axis=0
    )


def split(values):
    high = values.astype(BF16)
    low = (values - high.astype(F32)).astype(BF16)
    return high, low


def mm(a, b):
    return jnp.dot(a, b, preferred_element_type=F32)


def kernel(
    pairs, kb_hbm, g_ref, m_ref, tab_ref, nm_ref, total_ref, sums_ref,
    kb_ref, g_buf, m_buf, tab, masked, fold, spread, compact, tiles_x, tiles_y, sums_x,
    load_sem, kb_sem, send_sem, recv_sem, gather_send, gather_recv,
):
    width = pairs * LANES
    n_blocks = 2 * pairs
    replica, section = lax.axis_index("replica"), lax.axis_index("section")
    x = replica // (CHIPS_Y * CORES)
    y = (replica // CORES) % CHIPS_Y
    core = replica % CORES
    mine = x * CORES + core

    def peer(dx=0, dy=0, dc=0, dz=0):
        px, py, pc = (x + dx) % CHIPS_X, (y + dy) % CHIPS_Y, (core + dc) % CORES
        return ((px * CHIPS_Y + py) * CORES + pc, (section + dz) % SECTIONS)

    group_x = sorted([(dx, dc) for dx in range(CHIPS_X) for dc in range(CORES)][1:], key=lambda o: (-min(o[0], CHIPS_X - o[0]), -o[1]))
    group_y = sorted(range(1, CHIPS_Y), key=lambda d: -min(d, CHIPS_Y - d))
    group_z = sorted(range(1, SECTIONS), key=lambda d: -min(d, SECTIONS - d))

    half = OWNERS // 2 * width
    loads = []
    kb_load = pltpu.make_async_copy(kb_hbm, kb_ref, kb_sem)
    tab_load = pltpu.make_async_copy(tab_ref, tab, load_sem.at[4])
    for h in range(2):
        cols = slice(h * half, (h + 1) * half)
        pair = (
            pltpu.make_async_copy(m_ref.at[:, cols], m_buf.at[:, cols], load_sem.at[2 * h]),
            pltpu.make_async_copy(g_ref.at[:, cols], g_buf.at[:, cols], load_sem.at[2 * h + 1]),
        )
        loads.append(pair)
        pair[0].start()
        pair[1].start()
        if h == 0:
            kb_load.start()
            tab_load.start()

    barrier = pltpu.get_barrier_semaphore()
    everyone = (
        [peer(dx=dx, dc=dc) for dx, dc in group_x]
        + [peer(dy=d) for d in range(1, CHIPS_Y)]
        + [peer(dz=d) for d in range(1, SECTIONS)]
    )
    for other in everyone:
        pl.semaphore_signal(barrier, inc=1, device_id=other, device_id_type=MESH)

    lane8 = lax.broadcasted_iota(jnp.int32, (BLOCK, LANES), 1)
    row8 = lax.broadcasted_iota(jnp.int32, (BLOCK, LANES), 0)
    upper = lane8 >= GROUP
    lane_q = (lane8 % GROUP) // BLOCK
    row_g = lax.broadcasted_iota(jnp.int32, (LANES, LANES), 0)
    lane_g = lax.broadcasted_iota(jnp.int32, (LANES, LANES), 1)
    same_hm = (row_g // GROUP == lane_g // GROUP) & (row_g % BLOCK == lane_g % BLOCK)
    fold[...] = jnp.where(same_hm, 1.0, 0.0).astype(BF16)
    for i in range(BLOCK):
        of_row = same_hm & ((row_g % GROUP) // BLOCK == i)
        spread[:, i * LANES : (i + 1) * LANES] = jnp.where(of_row, 1.0, 0.0).astype(BF16)

    kb_load.wait()
    tab_load.wait()
    right_fwd = tab[0:384, :]
    right_inv = tab[384:768, :]
    left_fwd = jnp.concatenate([tab[768:832, :], tab[832:896, 0:64]], axis=1)
    left_inv = jnp.concatenate([tab[896:960, :], tab[960:1024, 0:64]], axis=1)
    left_inv_ip = jnp.concatenate([tab[1024:1088, :], tab[1088:1152, 0:64]], axis=1)

    def block_pair(s, j):
        c = s * n_blocks + 2 * j
        return kb_ref[0, c], kb_ref[0, c + 1]

    def p_lanes(s, j):
        k0, k1 = block_pair(s, j)
        return jnp.where(upper, k1 // SIDE, k0 // SIDE)

    def q_lanes(s, j):
        k0, k1 = block_pair(s, j)
        return jnp.where(upper, k1 % SIDE, k0 % SIDE)

    chosen = []
    for s in range(OWNERS):
        if s % (OWNERS // 2) == 0:
            for copy in loads[s // (OWNERS // 2)]:
                copy.wait()
        cols = slice(s * width, (s + 1) * width)
        moments = momentum_decay * m_buf[:, cols] + g_buf[:, cols].astype(F32)
        nm_ref[:, cols] = moments
        high, low = split(moments)
        rows = mm(left_fwd, jnp.concatenate([high, low, high], axis=0))
        for j in range(pairs):
            p_of = p_lanes(s, j)
            picked = jnp.zeros((BLOCK, LANES), F32)
            for p in range(SIDE):
                picked = jnp.where(p_of == p, rows[p * BLOCK : (p + 1) * BLOCK, j * LANES : (j + 1) * LANES], picked)
            chosen.append(picked)

    high, low = split(jnp.concatenate(chosen, axis=0))
    spectrum = mm(jnp.concatenate([high, low, high], axis=1), right_fwd)
    for s in range(OWNERS):
        for j in range(pairs):
            row = (s * pairs + j) * BLOCK
            masked[row : row + BLOCK, :] = jnp.where(q_lanes(s, j) == lane_q, spectrum[row : row + BLOCK, :], 0.0)

    kept_high, kept_low = split(masked[...])
    folded = mm(kept_high, fold[...]) + mm(kept_low, fold[...])
    for s in range(OWNERS):
        tile = jnp.zeros((BLOCK, LANES), F32)
        for j in range(pairs):
            row = (s * pairs + j) * BLOCK
            piece = jnp.where(row8 == lane_q, folded[row : row + BLOCK, :], 0.0)
            for shift in (4, 2, 1):
                piece = piece + pltpu.roll(piece, shift, 0)
            tile = jnp.where(row8 == j, piece, tile)
        for b in range(n_blocks):
            number = kb_ref[0, s * n_blocks + b].astype(F32)
            tile = jnp.where((row8 == pairs) & (lane8 == b), number, tile)
        compact[s] = tile

    pl.semaphore_wait(barrier, len(everyone))

    def send(src, dst, i, other):
        copy = pltpu.make_async_remote_copy(
            src_ref=src, dst_ref=dst, send_sem=send_sem.at[i], recv_sem=recv_sem.at[i],
            device_id=other, device_id_type=MESH,
        )
        copy.start()

    def all_of(ref, i):
        return pltpu.make_async_remote_copy(
            src_ref=ref, dst_ref=ref, send_sem=send_sem.at[i], recv_sem=recv_sem.at[i],
            device_id=peer(dc=1), device_id_type=MESH,
        )

    for i, (dx, dc) in enumerate(group_x, start=1):
        px, pc = (x + dx) % CHIPS_X, (core + dc) % CORES
        send(compact.at[px * CORES + pc], tiles_x.at[pl.ds(i * BLOCK, BLOCK)], 0, peer(dx=dx, dc=dc))
    tiles_x[0:BLOCK, :] = compact[mine]

    wide = mm(jnp.concatenate([kept_high, kept_low, kept_high], axis=1), right_inv)
    for s in range(OWNERS):
        cols = slice(s * width, (s + 1) * width)
        placed = []
        for j in range(pairs):
            p_of = p_lanes(s, j)
            row = (s * pairs + j) * BLOCK
            piece = wide[row : row + BLOCK, :]
            placed.append(jnp.concatenate([jnp.where(p_of == p, piece, 0.0) for p in range(SIDE)], axis=0))
        high, low = split(jnp.concatenate(placed, axis=1))
        nm_ref[:, cols] = nm_ref[:, cols] - mm(left_inv, jnp.concatenate([high, low, high], axis=0))

    all_of(tiles_x.at[BLOCK:], 0).wait_recv()

    n_x = OWNERS * BLOCK
    for d in group_y:
        send(tiles_x, tiles_y.at[pl.ds(d * n_x, n_x)], 1, peer(dy=d))
    tiles_y[0:n_x, :] = tiles_x[...]
    all_of(tiles_y.at[n_x:], 1).wait_recv()

    n_replica = CHIPS_Y * OWNERS
    numbers = tiles_y[pl.ds(pairs, n_replica, stride=BLOCK), :].astype(BF16)
    row_n = lax.broadcasted_iota(jnp.int32, (2 * BLOCK, LANES), 0)
    lane_n = lax.broadcasted_iota(jnp.int32, (2 * BLOCK, LANES), 1)
    pick = jnp.where(row_n == lane_n, 1.0, 0.0).astype(BF16)
    numbers = lax.dot_general(pick, numbers, (((1,), (1,)), ((), ())), preferred_element_type=F32)
    place = lax.broadcasted_iota(jnp.int32, (GROUP, n_replica), 0).astype(F32)
    lane64 = lax.broadcasted_iota(jnp.int32, (GROUP, LANES), 1)
    row64 = lax.broadcasted_iota(jnp.int32, (GROUP, LANES), 0)
    squares = jnp.zeros((BLOCK, LANES), F32)
    spectra = []
    for j in range(pairs):
        high, low = split(tiles_y[pl.ds(j, n_replica, stride=BLOCK), :])
        where_to = jnp.concatenate(
            [jnp.where(numbers[b : b + 1, :] == place, 1.0, 0.0).astype(BF16) for b in (2 * j, 2 * j + 1)], axis=0
        )
        both = mm(jnp.concatenate([where_to, where_to], axis=1), jnp.concatenate([high, low], axis=0))
        both = jnp.where(lane64 >= GROUP, both[GROUP:, :], both[:GROUP, :])
        spectra.append(both)
        for p in range(SIDE):
            piece = both[p * BLOCK : (p + 1) * BLOCK, :]
            squares = squares + piece * piece
    sums_x[0] = squares
    for i, (dx, dc) in enumerate(group_x, start=1):
        send(sums_x.at[0], sums_x.at[i], 2, peer(dx=dx, dc=dc))

    row_p = lax.broadcasted_iota(jnp.int32, (BLOCK, LANES), 0)
    gather_p = jnp.where((lane8 % GROUP) // SIDE == row_p, 1.0, 0.0).astype(BF16)
    same_q = row64 % SIDE == (lane64 % GROUP) // BLOCK
    stacked = []
    for j in range(pairs):
        high, low = split(spectra[j])
        both = mm(high, spread[...]) + mm(low, spread[...])
        both = jnp.concatenate(
            [jnp.where(same_q, both[:, i * LANES : (i + 1) * LANES], 0.0) for i in range(BLOCK)], axis=1
        )
        high, low = split(both)
        both = mm(gather_p, jnp.concatenate([high, low], axis=0))
        stacked += [both[:, i * LANES : (i + 1) * LANES] for i in range(BLOCK)]
    high, low = split(jnp.concatenate(stacked, axis=0))
    wide = mm(jnp.concatenate([high, low, high], axis=1), right_inv)
    high, low = split(jnp.concatenate([wide[j * GROUP : (j + 1) * GROUP, :] for j in range(pairs)], axis=1))
    total_ref[mine] = mm(left_inv_ip, jnp.concatenate([high, low, high], axis=0))

    def gather(slot, i, other):
        return pltpu.make_async_remote_copy(
            src_ref=total_ref.at[slot], dst_ref=total_ref.at[slot],
            send_sem=gather_send.at[i], recv_sem=gather_recv.at[i], device_id=other, device_id_type=MESH,
        )

    sends = [gather(mine, d, peer(dx=d)) for d in (1, 3, 2)] + [gather(mine, 4, peer(dc=1))]
    for copy in sends:
        copy.start()

    all_of(sums_x.at[1:OWNERS], 2).wait_recv()
    sums_ref[0] = jnp.sum(sums_x[...], axis=0)
    for d in group_z:
        send(sums_ref.at[0], sums_ref.at[d], 3, peer(dz=d))

    for d in (1, 3, 2):
        slot = ((x + CHIPS_X - d) % CHIPS_X) * CORES + core
        gather(slot, d, peer(dx=d)).wait_recv()
        copy = gather(slot, 4 + d, peer(dc=1))
        copy.start()
        sends.append(copy)
    for d in (0, 1, 3, 2):
        slot = ((x + CHIPS_X - d) % CHIPS_X) * CORES + (core + 1) % CORES
        gather(slot, 4 + d, peer(dc=1)).wait_recv()

    all_of(sums_ref.at[1:SECTIONS], 3).wait_recv()
    all_of(compact.at[1:OWNERS], 0).wait_send()
    all_of(tiles_y.at[n_x:], 1).wait_send()
    all_of(sums_x.at[1:OWNERS], 2).wait_send()
    all_of(sums_ref.at[1:SECTIONS], 3).wait_send()
    for copy in sends:
        copy.wait_send()


def finish(entry_count, width, nm_ref, total_ref, sums_ref, nm_out, upd_out, upd, sem):
    stores = [pltpu.make_async_copy(nm_ref, nm_out, sem.at[0])]
    stores[0].start()
    squares = jnp.sum(sums_ref[...], axis=0)
    squares = jnp.sum(jnp.sum(squares, axis=0, keepdims=True), axis=1, keepdims=True)
    scale = lax.rsqrt(squares / entry_count + epsilon)
    for k in range(OWNERS // 2):
        for s in (2 * k, 2 * k + 1):
            upd[:, s * width : (s + 1) * width] = (total_ref[s] * scale).astype(BF16)
        cols = slice(2 * k * width, 2 * (k + 1) * width)
        stores.append(pltpu.make_async_copy(upd.at[:, cols], upd_out.at[:, cols], sem.at[1 + k]))
        stores[-1].start()
    for copy in stores:
        copy.wait()


def per_device(gradients, momentum, keep_block):
    local_rows, columns = gradients.shape[1:]
    pairs = columns // (OWNERS * LANES)
    width = pairs * LANES
    tables = jnp.asarray(constant_tables())
    entry_count = float(local_rows * lax.axis_size("section") * columns)
    dma = pltpu.SemaphoreType.DMA
    new_momentum, total, sums = pl.pallas_call(
        functools.partial(kernel, pairs),
        out_shape=(
            pltpu.VMEM((local_rows, columns), F32),
            pltpu.VMEM((OWNERS, local_rows, width), F32),
            pltpu.VMEM((SECTIONS, BLOCK, LANES), F32),
        ),
        in_specs=[pl.BlockSpec(memory_space=pltpu.HBM)] * 4,
        out_specs=(pl.BlockSpec(memory_space=pltpu.VMEM),) * 3,
        scratch_shapes=[
            pltpu.SMEM(keep_block.shape[1:], jnp.int32),
            pltpu.VMEM((local_rows, columns), BF16),
            pltpu.VMEM((local_rows, columns), F32),
            pltpu.VMEM(tables.shape, BF16),
            pltpu.VMEM((OWNERS * pairs * BLOCK, LANES), F32),
            pltpu.VMEM((LANES, LANES), BF16),
            pltpu.VMEM((LANES, BLOCK * LANES), BF16),
            pltpu.VMEM((OWNERS, BLOCK, LANES), F32),
            pltpu.VMEM((OWNERS * BLOCK, LANES), F32),
            pltpu.VMEM((CHIPS_Y * OWNERS * BLOCK, LANES), F32),
            pltpu.VMEM((OWNERS, BLOCK, LANES), F32),
            dma((5,)), dma, dma((4,)), dma((4,)), dma((OWNERS,)), dma((OWNERS,)),
        ],
        compiler_params=pltpu.CompilerParams(collective_id=0, has_side_effects=True, vmem_limit_bytes=56 << 20),
        name="kept_blocks_step",
    )(keep_block[0], gradients[0], momentum[0], tables)
    hbm = pl.BlockSpec(memory_space=pltpu.HBM)
    new_momentum, update = pl.pallas_call(
        functools.partial(finish, entry_count, width),
        out_shape=(
            jax.ShapeDtypeStruct((local_rows, columns), F32),
            jax.ShapeDtypeStruct((local_rows, columns), BF16),
        ),
        in_specs=[pl.BlockSpec(memory_space=pltpu.VMEM)] * 3,
        out_specs=(hbm, hbm),
        scratch_shapes=[pltpu.VMEM((local_rows, columns), BF16), dma((1 + OWNERS // 2,))],
        compiler_params=pltpu.CompilerParams(vmem_limit_bytes=32 << 20),
        name="scale_and_store",
    )(new_momentum, total, sums)
    return new_momentum[None], update


def solution(mesh):
    placed = (
        P("replica", "section", None),
        P("replica", "section", None),
        P("replica", "section", None),
    )
    return jax.shard_map(
        per_device,
        mesh=mesh,
        in_specs=placed,
        out_specs=(P("replica", "section", None), P("section", None)),
        check_vma=False,
    )
```

```python
import functools

import jax
import jax.numpy as jnp
import ml_dtypes
import numpy as np
from jax import lax
from jax.experimental import pallas as pl
from jax.experimental.pallas import tpu as pltpu
from jax.sharding import PartitionSpec as P

GROUP = 64
BLOCK = 8
SIDE = GROUP // BLOCK
LANES = 128
CHIPS_X, CHIPS_Y, CORES, SECTIONS = 4, 8, 2, 8
OWNERS = CHIPS_X * CORES
MESH = pl.DeviceIdType.MESH
ROWS_SENT = 48
TOP = 32000.0
F32, BF16 = jnp.float32, jnp.bfloat16

momentum_decay = 0.9
epsilon = 1e-06


def dct_basis():
    k = np.arange(GROUP, dtype=np.float64)[:, None]
    n = np.arange(GROUP, dtype=np.float64)[None, :]
    basis = np.sqrt(2.0 / GROUP) * np.cos(np.pi * (2.0 * n + 1.0) * k / (2.0 * GROUP))
    basis[0] /= np.sqrt(2.0)
    return basis.astype(np.float32)


def two_terms(values):
    high = values.astype(ml_dtypes.bfloat16)
    low = (values - high.astype(np.float32)).astype(ml_dtypes.bfloat16)
    return high, low


def constant_tables():
    basis = dct_basis()

    def right(matrix):
        high, low = two_terms(np.kron(np.eye(2, dtype=np.float32), matrix))
        return np.concatenate([high, high, low], axis=0)

    def left(matrix):
        high, low = two_terms(matrix)
        wide = np.concatenate([high, high, low, np.zeros_like(low)], axis=1)
        return np.concatenate([wide[:, :LANES], wide[:, LANES:]], axis=0)

    by_row_in_block = np.arange(GROUP).reshape(SIDE, BLOCK).T.reshape(-1)
    return np.concatenate(
        [right(basis.T), right(basis), left(basis), left(basis.T), left(basis.T[:, by_row_in_block])], axis=0
    )


def column_table():
    basis = dct_basis().reshape(SIDE, BLOCK, GROUP)
    table = np.einsum("qmn,ij->qimjn", basis, np.eye(BLOCK, dtype=np.float32))
    terms = np.stack(two_terms(table.reshape(SIDE * GROUP, BLOCK * GROUP)))
    return terms.reshape(2, SIDE * GROUP, BLOCK * GROUP // LANES, LANES).transpose(0, 2, 1, 3).reshape(-1, LANES)


def split(values):
    high = values.astype(BF16)
    low = (values - high.astype(F32)).astype(BF16)
    return high, low


def mm(a, b):
    return jnp.dot(a, b, preferred_element_type=F32)


def kernel(
    pairs, kb_hbm, g_ref, m_ref, tab_ref, col_ref, nm_ref, total_ref, sums_ref,
    kb_ref, kb_row, g_buf, m_buf, tab, col_tab, masked, fold, tiles, wide_tiles, spec_high, spec_low, total_high, total_low,
    load_sem, kb_sem, send_sem, y_recv, x_recv, core_recv, z_recv,
):
    width = pairs * LANES
    n_blocks = 2 * pairs
    replica, section = lax.axis_index("replica"), lax.axis_index("section")
    x = replica // (CHIPS_Y * CORES)
    y = (replica // CORES) % CHIPS_Y
    core = replica % CORES

    def peer(dx=0, dy=0, dc=0, dz=0):
        px, py, pc = (x + dx) % CHIPS_X, (y + dy) % CHIPS_Y, (core + dc) % CORES
        return ((px * CHIPS_Y + py) * CORES + pc, (section + dz) % SECTIONS)

    n_pairs = OWNERS * pairs
    group_y = sorted(range(1, CHIPS_Y), key=lambda d: -min(d, CHIPS_Y - d))
    group_x = (2, 1, 3)
    row_order = (0, 2, 3, 1, 6, 7, 5, 4)

    half = OWNERS // 2 * width
    loads = []
    kb_load = pltpu.make_async_copy(kb_hbm, kb_ref, kb_sem.at[0])
    kb_row_load = pltpu.make_async_copy(kb_hbm, kb_row, kb_sem.at[1])
    tab_load = pltpu.make_async_copy(tab_ref, tab, load_sem.at[4])
    for h in range(2):
        cols = slice(h * half, (h + 1) * half)
        pair = (
            pltpu.make_async_copy(m_ref.at[:, cols], m_buf.at[:, cols], load_sem.at[2 * h]),
            pltpu.make_async_copy(g_ref.at[:, cols], g_buf.at[:, cols], load_sem.at[2 * h + 1]),
        )
        loads.append(pair)
        pair[0].start()
        pair[1].start()
        if h == 0:
            kb_load.start()
            kb_row_load.start()
            tab_load.start()

    col_load = pltpu.make_async_copy(col_ref, col_tab, load_sem.at[5])
    col_load.start()

    barrier = pltpu.get_barrier_semaphore()
    everyone = (
        [peer(dx=d) for d in group_x]
        + [peer(dy=d) for d in group_y]
        + [peer(dz=d) for d in range(1, SECTIONS)]
        + [peer(dc=1)]
    )
    for other in everyone:
        pl.semaphore_signal(barrier, inc=1, device_id=other, device_id_type=MESH)

    lane8 = lax.broadcasted_iota(jnp.int32, (BLOCK, LANES), 1)
    row8 = lax.broadcasted_iota(jnp.int32, (BLOCK, LANES), 0)
    upper = lane8 >= GROUP
    lane_q = (lane8 % GROUP) // BLOCK
    row_g = lax.broadcasted_iota(jnp.int32, (LANES, LANES), 0)
    lane_g = lax.broadcasted_iota(jnp.int32, (LANES, LANES), 1)
    same_hm = (row_g // GROUP == lane_g // GROUP) & (row_g % BLOCK == lane_g % BLOCK)
    fold[...] = jnp.where(same_hm, 1.0, 0.0).astype(BF16)

    kb_load.wait()
    kb_row_load.wait()
    numbers = jnp.concatenate([kb_row[...].astype(F32), jnp.zeros((1, LANES - kb_row.shape[1]), F32)], axis=1)
    tab_load.wait()
    right_fwd = tab[0:384, :]
    right_inv = tab[384:768, :]
    left_fwd = jnp.concatenate([tab[768:832, :], tab[832:896, 0:64]], axis=1)
    left_inv = jnp.concatenate([tab[896:960, :], tab[960:1024, 0:64]], axis=1)
    left_inv_ip = jnp.concatenate([tab[1024:1088, :], tab[1088:1152, 0:64]], axis=1)

    def block_pair(s, j):
        c = s * n_blocks + 2 * j
        return kb_ref[0, c], kb_ref[0, c + 1]

    def p_lanes(s, j):
        k0, k1 = block_pair(s, j)
        return jnp.where(upper, k1 // SIDE, k0 // SIDE)

    def q_lanes(s, j):
        k0, k1 = block_pair(s, j)
        return jnp.where(upper, k1 % SIDE, k0 % SIDE)

    chosen = []
    for s in range(OWNERS):
        if s % (OWNERS // 2) == 0:
            for copy in loads[s // (OWNERS // 2)]:
                copy.wait()
        cols = slice(s * width, (s + 1) * width)
        moments = momentum_decay * m_buf[:, cols] + g_buf[:, cols].astype(F32)
        nm_ref[:, cols] = moments
        high, low = split(moments)
        rows = mm(left_fwd, jnp.concatenate([high, low, high], axis=0))
        for j in range(pairs):
            p_of = p_lanes(s, j)
            picked = jnp.zeros((BLOCK, LANES), F32)
            for p in range(SIDE):
                picked = jnp.where(p_of == p, rows[p * BLOCK : (p + 1) * BLOCK, j * LANES : (j + 1) * LANES], picked)
            chosen.append(picked)

    high, low = split(jnp.concatenate(chosen, axis=0))
    spectrum = mm(jnp.concatenate([high, low, high], axis=1), right_fwd)
    for s in range(OWNERS):
        for j in range(pairs):
            row = (s * pairs + j) * BLOCK
            masked[row : row + BLOCK, :] = jnp.where(q_lanes(s, j) == lane_q, spectrum[row : row + BLOCK, :], 0.0)

    kept_high, kept_low = split(masked[...])
    folded = mm(kept_high, fold[...]) + mm(kept_low, fold[...])
    lines = []
    for k in range(n_pairs):
        piece = jnp.where(row8 == lane_q, folded[k * BLOCK : (k + 1) * BLOCK, :], 0.0)
        for shift in (4, 2, 1):
            piece = piece + pltpu.roll(piece, shift, 0)
        if k % BLOCK == 0:
            lines.append(piece)
        else:
            lines[-1] = jnp.where(row8 == k % BLOCK, piece, lines[-1])

    largest = jnp.abs(lines[0])
    for line in lines[1:]:
        largest = jnp.maximum(largest, jnp.abs(line))
    largest = jnp.max(jnp.max(largest, axis=0, keepdims=True), axis=1, keepdims=True)
    exponent = jnp.ceil(jnp.log2(jnp.maximum(largest, 1e-30)) + 0.01)
    to_code = TOP * jnp.exp2(-exponent)
    coded = [jnp.round(line * to_code) for line in lines]
    coded.append(jnp.where(row8 == 0, numbers, jnp.where(row8 == 1, exponent, 0.0)))
    coded = jnp.concatenate(coded, axis=0).astype(jnp.int32).astype(jnp.int16)
    tiles[y, core, 0] = coded

    pl.semaphore_wait(barrier, len(everyone))

    SEND_Y, SEND_X, SEND_CORE, SEND_Z = range(4)

    def remote(src, dst, which, recv, other):
        return pltpu.make_async_remote_copy(
            src_ref=src, dst_ref=dst, send_sem=send_sem.at[which], recv_sem=recv, device_id=other, device_id_type=MESH
        )

    def received(ref, recv):
        remote(ref, ref, SEND_Y, recv, peer(dc=1)).wait_recv()

    def sent(ref, which):
        remote(ref, ref, which, z_recv, peer(dc=1)).wait_send()

    def along_x(row):
        for d in group_x:
            remote(tiles.at[row, core, 0], tiles.at[row, core, CHIPS_X - d], SEND_X, x_recv.at[row], peer(dx=d)).start()

    def to_core(row):
        received(tiles.at[row, core, 1:CHIPS_X], x_recv.at[row])
        remote(tiles.at[row, core], tiles.at[row, core], SEND_CORE, core_recv.at[row], peer(dc=1)).start()

    for d in group_y:
        remote(tiles.at[y, core, 0], tiles.at[y, core, 0], SEND_Y, y_recv.at[y], peer(dy=d)).start()
    along_x(y)

    wide = mm(jnp.concatenate([kept_high, kept_low, kept_high], axis=1), right_inv)
    for s in range(OWNERS):
        cols = slice(s * width, (s + 1) * width)
        placed = []
        for j in range(pairs):
            p_of = p_lanes(s, j)
            row = (s * pairs + j) * BLOCK
            piece = wide[row : row + BLOCK, :]
            placed.append(jnp.concatenate([jnp.where(p_of == p, piece, 0.0) for p in range(SIDE)], axis=0))
        high, low = split(jnp.concatenate(placed, axis=1))
        nm_ref[:, cols] = nm_ref[:, cols] - mm(left_inv, jnp.concatenate([high, low, high], axis=0))

    lag = 4
    for k in range(CHIPS_Y + lag):
        if k < CHIPS_Y:
            row = row_order[k]

            @pl.when(y != row)
            def _():
                received(tiles.at[row, core, 0], y_recv.at[row])
                along_x(row)

        if k >= lag:
            to_core(row_order[k - lag])
    n_replica = CHIPS_Y * CORES * CHIPS_X
    of_row = CORES * CHIPS_X * ROWS_SENT
    for row in row_order:
        received(tiles.at[row, 1 - core], core_recv.at[row])
        values = tiles[row].reshape(of_row, LANES).astype(jnp.int32).astype(F32)
        wide_tiles[row * of_row : (row + 1) * of_row, :] = values

    def halves(tiles_of):
        firsts, seconds = [], []
        for even, odd in zip(tiles_of[0::2], tiles_of[1::2]):
            firsts.append(jnp.where(upper, pltpu.roll(odd, GROUP, 1), even))
            seconds.append(jnp.where(upper, odd, pltpu.roll(even, GROUP, 1)))
        return jnp.concatenate([jnp.concatenate(firsts, axis=1), jnp.concatenate(seconds, axis=1)], axis=0)

    def of_all(line):
        return wide_tiles[pl.ds(line, n_replica, stride=ROWS_SENT), :]

    row_n = lax.broadcasted_iota(jnp.int32, (2 * n_pairs, LANES), 0)
    lane_n = lax.broadcasted_iota(jnp.int32, (2 * n_pairs, LANES), 1)
    pick = jnp.where(row_n == lane_n, 1.0, 0.0).astype(BF16)
    numbers = lax.dot_general(
        pick, of_all(n_pairs).astype(BF16), (((1,), (1,)), ((), ())), preferred_element_type=F32
    )
    from_code = jnp.exp2(of_all(n_pairs + 1)) * (1.0 / TOP)
    row_place = lax.broadcasted_iota(jnp.int32, (GROUP, n_replica), 0)
    place = ((row_place % BLOCK) * SIDE + row_place // BLOCK).astype(F32)
    lane64 = lax.broadcasted_iota(jnp.int32, (GROUP, LANES), 1)
    squares = jnp.zeros((BLOCK, LANES), F32)
    for k in range(n_pairs):
        high, low = split(of_all(k) * from_code)
        where_to = jnp.concatenate(
            [jnp.where(numbers[b : b + 1, :] == place, 1.0, 0.0).astype(BF16) for b in (2 * k, 2 * k + 1)], axis=0
        )
        both = mm(jnp.concatenate([where_to, where_to], axis=1), jnp.concatenate([high, low], axis=0))
        both = jnp.where(lane64 >= GROUP, both[GROUP:, :], both[:GROUP, :])
        by_q = [both[q * BLOCK : (q + 1) * BLOCK, :] for q in range(SIDE)]
        for piece in by_q:
            squares = squares + piece * piece
        high, low = split(halves(by_q))
        spec_high[k * 2 * BLOCK : (k + 1) * 2 * BLOCK, :] = high
        spec_low[k * 2 * BLOCK : (k + 1) * 2 * BLOCK, :] = low
    sums_ref[0] = squares
    for other in range(SECTIONS):

        @pl.when(section != other)
        def _():
            d = (other - section + SECTIONS) % SECTIONS
            remote(sums_ref.at[0], sums_ref.at[d], SEND_Z, z_recv, (replica, other)).start()

    col_load.wait()
    tall = SIDE * GROUP
    pieces = [col_tab[i * tall : (i + 1) * tall, :] for i in range(2 * BLOCK * GROUP // LANES)]
    col_high = jnp.concatenate(pieces[: len(pieces) // 2], axis=1)
    col_low = jnp.concatenate(pieces[len(pieces) // 2 :], axis=1)
    for s in range(OWNERS):
        part = slice(s * pairs * 2 * BLOCK, (s + 1) * pairs * 2 * BLOCK)
        cols = slice(s * width, (s + 1) * width)
        high, low = spec_high[part, :], spec_low[part, :]
        wide = mm(high, col_high) + mm(low, col_high) + mm(high, col_low)
        stacked = []
        for j in range(pairs):
            first = [wide[2 * j * BLOCK : (2 * j + 1) * BLOCK, a * LANES : (a + 1) * LANES] for a in range(BLOCK // 2)]
            second = [wide[(2 * j + 1) * BLOCK : (2 * j + 2) * BLOCK, a * LANES : (a + 1) * LANES] for a in range(BLOCK // 2)]
            by_i = []
            for a, b in zip(first, second):
                by_i.append(jnp.where(upper, pltpu.roll(b, GROUP, 1), a))
                by_i.append(jnp.where(upper, b, pltpu.roll(a, GROUP, 1)))
            stacked.append(jnp.concatenate(by_i, axis=0))
        high, low = split(jnp.concatenate(stacked, axis=1))
        total_high[:, cols] = high
        total_low[:, cols] = low
    for s in range(OWNERS):
        cols = slice(s * width, (s + 1) * width)
        high, low = total_high[:, cols], total_low[:, cols]
        total_ref[:, cols] = mm(left_inv_ip, jnp.concatenate([high, low, high], axis=0))

    received(sums_ref.at[1:SECTIONS], z_recv)

    n_y = (CHIPS_Y - 1) * ROWS_SENT // 2
    sent(wide_tiles.at[0:n_y], SEND_Y)
    sent(tiles.at[0:3], SEND_X)
    sent(tiles.at[0:4], SEND_CORE)
    sent(sums_ref.at[1:SECTIONS], SEND_Z)


def finish(entry_count, width, nm_ref, total_ref, sums_ref, nm_out, upd_out, upd, sem):
    stores = [pltpu.make_async_copy(nm_ref, nm_out, sem.at[0])]
    stores[0].start()
    squares = jnp.sum(sums_ref[...], axis=0)
    squares = jnp.sum(jnp.sum(squares, axis=0, keepdims=True), axis=1, keepdims=True)
    scale = lax.rsqrt(squares / entry_count + epsilon)
    for k in range(OWNERS // 2):
        for s in (2 * k, 2 * k + 1):
            upd[:, s * width : (s + 1) * width] = (total_ref[:, s * width : (s + 1) * width] * scale).astype(BF16)
        cols = slice(2 * k * width, 2 * (k + 1) * width)
        stores.append(pltpu.make_async_copy(upd.at[:, cols], upd_out.at[:, cols], sem.at[1 + k]))
        stores[-1].start()
    for copy in stores:
        copy.wait()


def per_device(gradients, momentum, keep_block):
    local_rows, columns = gradients.shape[1:]
    pairs = columns // (OWNERS * LANES)
    width = pairs * LANES
    tables = jnp.asarray(constant_tables())
    col_table = jnp.asarray(column_table())
    entry_count = float(local_rows * lax.axis_size("section") * columns)
    dma = pltpu.SemaphoreType.DMA
    new_momentum, total, sums = pl.pallas_call(
        functools.partial(kernel, pairs),
        out_shape=(
            pltpu.VMEM((local_rows, columns), F32),
            pltpu.VMEM((local_rows, columns), F32),
            pltpu.VMEM((SECTIONS, BLOCK, LANES), F32),
        ),
        in_specs=[pl.BlockSpec(memory_space=pltpu.HBM)] * 5,
        out_specs=(pl.BlockSpec(memory_space=pltpu.VMEM),) * 3,
        scratch_shapes=[
            pltpu.SMEM(keep_block.shape[1:], jnp.int32),
            pltpu.VMEM(keep_block.shape[1:], jnp.int32),
            pltpu.VMEM((local_rows, columns), BF16),
            pltpu.VMEM((local_rows, columns), F32),
            pltpu.VMEM(tables.shape, BF16),
            pltpu.VMEM(col_table.shape, BF16),
            pltpu.VMEM((OWNERS * pairs * BLOCK, LANES), F32),
            pltpu.VMEM((LANES, LANES), BF16),
            pltpu.VMEM((CHIPS_Y, CORES, CHIPS_X, ROWS_SENT, LANES), jnp.int16),
            pltpu.VMEM((CHIPS_Y * CORES * CHIPS_X * ROWS_SENT, LANES), F32),
            pltpu.VMEM((OWNERS * pairs * 2 * BLOCK, SIDE * GROUP), BF16),
            pltpu.VMEM((OWNERS * pairs * 2 * BLOCK, SIDE * GROUP), BF16),
            pltpu.VMEM((local_rows, columns), BF16),
            pltpu.VMEM((local_rows, columns), BF16),
            dma((6,)), dma((2,)), dma((4,)), dma((CHIPS_Y,)), dma((CHIPS_Y,)), dma((CHIPS_Y,)), dma,
        ],
        compiler_params=pltpu.CompilerParams(collective_id=0, has_side_effects=True, vmem_limit_bytes=56 << 20),
        name="kept_blocks_step",
    )(keep_block[0], gradients[0], momentum[0], tables, col_table)
    hbm = pl.BlockSpec(memory_space=pltpu.HBM)
    new_momentum, update = pl.pallas_call(
        functools.partial(finish, entry_count, width),
        out_shape=(
            jax.ShapeDtypeStruct((local_rows, columns), F32),
            jax.ShapeDtypeStruct((local_rows, columns), BF16),
        ),
        in_specs=[pl.BlockSpec(memory_space=pltpu.VMEM)] * 3,
        out_specs=(hbm, hbm),
        scratch_shapes=[pltpu.VMEM((local_rows, columns), BF16), dma((1 + OWNERS // 2,))],
        compiler_params=pltpu.CompilerParams(vmem_limit_bytes=32 << 20),
        name="scale_and_store",
    )(new_momentum, total, sums)
    return new_momentum[None], update


def solution(mesh):
    placed = (
        P("replica", "section", None),
        P("replica", "section", None),
        P("replica", "section", None),
    )
    return jax.shard_map(
        per_device,
        mesh=mesh,
        in_specs=placed,
        out_specs=(P("replica", "section", None), P("section", None)),
        check_vma=False,
    )
```

```python
import functools

import jax
import jax.numpy as jnp
import ml_dtypes
import numpy as np
from jax import lax
from jax.experimental import pallas as pl
from jax.experimental.pallas import tpu as pltpu
from jax.sharding import PartitionSpec as P

GROUP = 64
BLOCK = 8
SIDE = GROUP // BLOCK
LANES = 128
CHIPS_X, CHIPS_Y, CORES, SECTIONS = 4, 8, 2, 8
OWNERS = CHIPS_X * CORES
MESH = pl.DeviceIdType.MESH
ROWS_SENT = 48
TOP_BITS = 15
F32, BF16 = jnp.float32, jnp.bfloat16

momentum_decay = 0.9
epsilon = 1e-06


def dct_basis():
    k = np.arange(GROUP, dtype=np.float64)[:, None]
    n = np.arange(GROUP, dtype=np.float64)[None, :]
    basis = np.sqrt(2.0 / GROUP) * np.cos(np.pi * (2.0 * n + 1.0) * k / (2.0 * GROUP))
    basis[0] /= np.sqrt(2.0)
    return basis.astype(np.float32)


def two_terms(values):
    high = values.astype(ml_dtypes.bfloat16)
    low = (values - high.astype(np.float32)).astype(ml_dtypes.bfloat16)
    return high, low


def constant_tables():
    basis = dct_basis()

    def right(matrix):
        high, low = two_terms(np.kron(np.eye(2, dtype=np.float32), matrix))
        return np.concatenate([high, high, low], axis=0)

    def left(matrix):
        high, low = two_terms(matrix)
        wide = np.concatenate([high, high, low, np.zeros_like(low)], axis=1)
        return np.concatenate([wide[:, :LANES], wide[:, LANES:]], axis=0)

    by_row_in_block = np.arange(GROUP).reshape(SIDE, BLOCK).T.reshape(-1)
    return np.concatenate(
        [right(basis.T), right(basis), left(basis), left(basis.T), left(basis.T[:, by_row_in_block])], axis=0
    )


def column_table():
    basis = dct_basis().reshape(SIDE, BLOCK, GROUP)
    table = np.einsum("qmn,ij->qimjn", basis, np.eye(BLOCK, dtype=np.float32))
    terms = np.stack(two_terms(table.reshape(SIDE * GROUP, BLOCK * GROUP)))
    return terms.reshape(2, SIDE * GROUP, BLOCK * GROUP // LANES, LANES).transpose(0, 2, 1, 3).reshape(-1, LANES)


def split(values):
    high = values.astype(BF16)
    low = (values - high.astype(F32)).astype(BF16)
    return high, low


def mm(a, b):
    return jnp.dot(a, b, preferred_element_type=F32)


def kernel(
    pairs, kb_hbm, g_ref, m_ref, tab_ref, col_ref, nm_ref, total_ref, sums_ref,
    kb_ref, kb_row, g_buf, m_buf, tab, col_tab, masked, fold, tiles, wide_tiles, spectra, spec_high, spec_low, wide_cols, total_high, total_low,
    load_sem, kb_sem, send_sem, y_recv, x_recv, core_recv, z_recv,
):
    width = pairs * LANES
    n_blocks = 2 * pairs
    replica, section = lax.axis_index("replica"), lax.axis_index("section")
    x = replica // (CHIPS_Y * CORES)
    y = (replica // CORES) % CHIPS_Y
    core = replica % CORES

    def peer(dx=0, dy=0, dc=0, dz=0):
        px, py, pc = (x + dx) % CHIPS_X, (y + dy) % CHIPS_Y, (core + dc) % CORES
        return ((px * CHIPS_Y + py) * CORES + pc, (section + dz) % SECTIONS)

    n_pairs = OWNERS * pairs
    group_y = sorted(range(1, CHIPS_Y), key=lambda d: -min(d, CHIPS_Y - d))
    group_x = (2, 1, 3)
    row_order = (0, 2, 3, 1, 6, 7, 5, 4)

    half = OWNERS // 2 * width
    loads = []
    kb_load = pltpu.make_async_copy(kb_hbm, kb_ref, kb_sem.at[0])
    kb_row_load = pltpu.make_async_copy(kb_hbm, kb_row, kb_sem.at[1])
    tab_load = pltpu.make_async_copy(tab_ref, tab, load_sem.at[4])
    for h in range(2):
        cols = slice(h * half, (h + 1) * half)
        pair = (
            pltpu.make_async_copy(m_ref.at[:, cols], m_buf.at[:, cols], load_sem.at[2 * h]),
            pltpu.make_async_copy(g_ref.at[:, cols], g_buf.at[:, cols], load_sem.at[2 * h + 1]),
        )
        loads.append(pair)
        pair[0].start()
        pair[1].start()
        if h == 0:
            kb_load.start()
            kb_row_load.start()
            tab_load.start()

    col_load = pltpu.make_async_copy(col_ref, col_tab, load_sem.at[5])

    barrier = pltpu.get_barrier_semaphore()
    everyone = (
        [peer(dx=d) for d in group_x]
        + [peer(dy=d) for d in group_y]
        + [peer(dz=d) for d in range(1, SECTIONS)]
        + [peer(dc=1)]
    )
    for other in everyone:
        pl.semaphore_signal(barrier, inc=1, device_id=other, device_id_type=MESH)

    lane8 = lax.broadcasted_iota(jnp.int32, (BLOCK, LANES), 1)
    row8 = lax.broadcasted_iota(jnp.int32, (BLOCK, LANES), 0)
    upper = lane8 >= GROUP
    lane_q = (lane8 % GROUP) // BLOCK
    row_g = lax.broadcasted_iota(jnp.int32, (LANES, LANES), 0)
    lane_g = lax.broadcasted_iota(jnp.int32, (LANES, LANES), 1)
    same_hm = (row_g // GROUP == lane_g // GROUP) & (row_g % BLOCK == lane_g % BLOCK)
    fold[...] = jnp.where(same_hm, 1.0, 0.0).astype(BF16)

    kb_load.wait()
    kb_row_load.wait()
    numbers = jnp.concatenate([kb_row[...].astype(F32), jnp.zeros((1, LANES - kb_row.shape[1]), F32)], axis=1)
    tab_load.wait()
    right_fwd = tab[0:384, :]
    right_inv = tab[384:768, :]
    left_fwd = jnp.concatenate([tab[768:832, :], tab[832:896, 0:64]], axis=1)
    left_inv = jnp.concatenate([tab[896:960, :], tab[960:1024, 0:64]], axis=1)
    left_inv_ip = jnp.concatenate([tab[1024:1088, :], tab[1088:1152, 0:64]], axis=1)

    def block_pair(s, j):
        c = s * n_blocks + 2 * j
        return kb_ref[0, c], kb_ref[0, c + 1]

    def p_lanes(s, j):
        k0, k1 = block_pair(s, j)
        return jnp.where(upper, k1 // SIDE, k0 // SIDE)

    def q_lanes(s, j):
        k0, k1 = block_pair(s, j)
        return jnp.where(upper, k1 % SIDE, k0 % SIDE)

    chosen = []
    for s in range(OWNERS):
        if s % (OWNERS // 2) == 0:
            for copy in loads[s // (OWNERS // 2)]:
                copy.wait()
        cols = slice(s * width, (s + 1) * width)
        moments = momentum_decay * m_buf[:, cols] + g_buf[:, cols].astype(F32)
        nm_ref[:, cols] = moments
        high, low = split(moments)
        rows = mm(left_fwd, jnp.concatenate([high, low, high], axis=0))
        for j in range(pairs):
            p_of = p_lanes(s, j)
            picked = jnp.zeros((BLOCK, LANES), F32)
            for p in range(SIDE):
                picked = jnp.where(p_of == p, rows[p * BLOCK : (p + 1) * BLOCK, j * LANES : (j + 1) * LANES], picked)
            chosen.append(picked)

    col_load.start()

    high, low = split(jnp.concatenate(chosen, axis=0))
    spectrum = mm(jnp.concatenate([high, low, high], axis=1), right_fwd)
    for s in range(OWNERS):
        for j in range(pairs):
            row = (s * pairs + j) * BLOCK
            masked[row : row + BLOCK, :] = jnp.where(q_lanes(s, j) == lane_q, spectrum[row : row + BLOCK, :], 0.0)

    kept_high, kept_low = split(masked[...])
    folded = mm(kept_high, fold[...]) + mm(kept_low, fold[...])
    lines = []
    for k in range(n_pairs):
        piece = jnp.where(row8 == lane_q, folded[k * BLOCK : (k + 1) * BLOCK, :], 0.0)
        for shift in (4, 2, 1):
            piece = piece + pltpu.roll(piece, shift, 0)
        if k % BLOCK == 0:
            lines.append(piece)
        else:
            lines[-1] = jnp.where(row8 == k % BLOCK, piece, lines[-1])

    largest = jnp.abs(lines[0])
    for line in lines[1:]:
        largest = jnp.maximum(largest, jnp.abs(line))
    largest = jnp.max(jnp.max(largest, axis=0, keepdims=True), axis=1, keepdims=True)
    exponent = jnp.ceil(jnp.log2(jnp.maximum(largest, 1e-30)) + 0.01)
    to_code = jnp.exp2(TOP_BITS - exponent)
    coded = [jnp.round(line * to_code) for line in lines]
    coded.append(jnp.where(row8 == 0, numbers, jnp.where(row8 == 1, exponent, 0.0)))
    coded = jnp.concatenate(coded, axis=0).astype(jnp.int32).astype(jnp.int16)
    tiles[y, core, 0] = coded

    pl.semaphore_wait(barrier, len(everyone))

    SEND_Y, SEND_X, SEND_CORE, SEND_Z = range(4)

    def remote(src, dst, which, recv, other):
        return pltpu.make_async_remote_copy(
            src_ref=src, dst_ref=dst, send_sem=send_sem.at[which], recv_sem=recv, device_id=other, device_id_type=MESH
        )

    def received(ref, recv):
        remote(ref, ref, SEND_Y, recv, peer(dc=1)).wait_recv()

    def sent(ref, which):
        remote(ref, ref, which, z_recv, peer(dc=1)).wait_send()

    def along_x(row):
        for d in group_x:
            remote(tiles.at[row, core, 0], tiles.at[row, core, CHIPS_X - d], SEND_X, x_recv.at[row], peer(dx=d)).start()

    def to_core(row):
        received(tiles.at[row, core, 1:CHIPS_X], x_recv.at[row])
        remote(tiles.at[row, core], tiles.at[row, core], SEND_CORE, core_recv.at[row], peer(dc=1)).start()

    for d in group_y:
        remote(tiles.at[y, core, 0], tiles.at[y, core, 0], SEND_Y, y_recv.at[y], peer(dy=d)).start()
    along_x(y)

    wide = mm(jnp.concatenate([kept_high, kept_low, kept_high], axis=1), right_inv)
    for s in range(OWNERS):
        cols = slice(s * width, (s + 1) * width)
        placed = []
        for j in range(pairs):
            p_of = p_lanes(s, j)
            row = (s * pairs + j) * BLOCK
            piece = wide[row : row + BLOCK, :]
            placed.append(jnp.concatenate([jnp.where(p_of == p, piece, 0.0) for p in range(SIDE)], axis=0))
        high, low = split(jnp.concatenate(placed, axis=1))
        nm_ref[:, cols] = nm_ref[:, cols] - mm(left_inv, jnp.concatenate([high, low, high], axis=0))

    lag = 7
    for k in range(CHIPS_Y + lag):
        if k < CHIPS_Y:
            row = row_order[k]

            @pl.when(y != row)
            def _():
                received(tiles.at[row, core, 0], y_recv.at[row])
                along_x(row)

        if k >= lag:
            to_core(row_order[k - lag])
    n_replica = CHIPS_Y * CORES * CHIPS_X
    of_row = CORES * CHIPS_X * ROWS_SENT
    for row in row_order:
        received(tiles.at[row, 1 - core], core_recv.at[row])
        values = tiles[row].reshape(of_row, LANES).astype(jnp.int32).astype(F32)
        wide_tiles[row * of_row : (row + 1) * of_row, :] = values

    def halves(tiles_of):
        firsts, seconds = [], []
        for even, odd in zip(tiles_of[0::2], tiles_of[1::2]):
            firsts.append(jnp.where(upper, pltpu.roll(odd, GROUP, 1), even))
            seconds.append(jnp.where(upper, odd, pltpu.roll(even, GROUP, 1)))
        return jnp.concatenate([jnp.concatenate(firsts, axis=1), jnp.concatenate(seconds, axis=1)], axis=0)

    def of_all(line):
        return wide_tiles[pl.ds(line, n_replica, stride=ROWS_SENT), :]

    def across(lines, rows):
        return lax.dot_general(rows, lines.astype(BF16), (((1,), (1,)), ((), ())), preferred_element_type=F32)

    row_n = lax.broadcasted_iota(jnp.int32, (n_pairs, LANES), 0)
    lane_n = lax.broadcasted_iota(jnp.int32, (n_pairs, LANES), 1)
    of_numbers = of_all(n_pairs)
    numbers = jnp.concatenate(
        [across(of_numbers, jnp.where(lane_n == 2 * row_n + h, 1.0, 0.0).astype(BF16)) for h in range(2)], axis=1
    )
    exponents = across(of_all(n_pairs + 1), jnp.where(lane8 == 0, 1.0, 0.0).astype(BF16))[0:1, :]
    from_code = jnp.exp2(jnp.concatenate([exponents, exponents], axis=1) - TOP_BITS)
    row_place = lax.broadcasted_iota(jnp.int32, (GROUP, LANES), 0)
    place = ((row_place % BLOCK) * SIDE + row_place // BLOCK).astype(F32)
    lane64 = lax.broadcasted_iota(jnp.int32, (GROUP, LANES), 1)
    of_first = jnp.where(lane64 < GROUP, 1.0, 0.0).astype(BF16)
    of_second = jnp.where(lane64 < GROUP, 0.0, 1.0).astype(BF16)
    squares = jnp.zeros((BLOCK, LANES), F32)
    for k in range(n_pairs):
        high, low = split(of_all(k))
        where_to = jnp.where(numbers[k : k + 1, :] == place, from_code, 0.0).astype(BF16)
        both = mm(
            jnp.concatenate([where_to, where_to], axis=1),
            jnp.concatenate([high * of_first, high * of_second, low * of_first, low * of_second], axis=0),
        )
        spectra[k * GROUP : (k + 1) * GROUP, :] = both
        for q in range(SIDE):
            piece = both[q * BLOCK : (q + 1) * BLOCK, :]
            squares = squares + piece * piece
    sums_ref[0] = squares
    for other in range(SECTIONS):

        @pl.when(section != other)
        def _():
            d = (other - section + SECTIONS) % SECTIONS
            remote(sums_ref.at[0], sums_ref.at[d], SEND_Z, z_recv, (replica, other)).start()

    col_load.wait()
    tall = SIDE * GROUP
    pieces = [col_tab[i * tall : (i + 1) * tall, :] for i in range(2 * BLOCK * GROUP // LANES)]
    col_high = jnp.concatenate(pieces[: len(pieces) // 2], axis=1)
    col_low = jnp.concatenate(pieces[len(pieces) // 2 :], axis=1)
    for k in range(n_pairs):
        by_q = [spectra[k * GROUP + q * BLOCK : k * GROUP + (q + 1) * BLOCK, :] for q in range(SIDE)]
        high, low = split(halves(by_q))
        spec_high[k * 2 * BLOCK : (k + 1) * 2 * BLOCK, :] = high
        spec_low[k * 2 * BLOCK : (k + 1) * 2 * BLOCK, :] = low
    for side in range(2):
        half_cols = slice(side * 2 * LANES, (side + 1) * 2 * LANES)
        wide_cols[...] = (
            mm(spec_high[...], col_high[:, half_cols])
            + mm(spec_low[...], col_high[:, half_cols])
            + mm(spec_high[...], col_low[:, half_cols])
        )
        for k in range(n_pairs):
            by_i = []
            for a in range(2):
                lanes = slice(a * LANES, (a + 1) * LANES)
                first = wide_cols[2 * k * BLOCK : (2 * k + 1) * BLOCK, lanes]
                second = wide_cols[(2 * k + 1) * BLOCK : (2 * k + 2) * BLOCK, lanes]
                by_i.append(jnp.where(upper, pltpu.roll(second, GROUP, 1), first))
                by_i.append(jnp.where(upper, second, pltpu.roll(first, GROUP, 1)))
            high, low = split(jnp.concatenate(by_i, axis=0))
            rows = slice(side * GROUP // 2, (side + 1) * GROUP // 2)
            total_high[rows, k * LANES : (k + 1) * LANES] = high
            total_low[rows, k * LANES : (k + 1) * LANES] = low
    for s in range(OWNERS):
        cols = slice(s * width, (s + 1) * width)
        high, low = total_high[:, cols], total_low[:, cols]
        total_ref[:, cols] = mm(left_inv_ip, jnp.concatenate([high, low, high], axis=0))

    received(sums_ref.at[1:SECTIONS], z_recv)

    n_y = (CHIPS_Y - 1) * ROWS_SENT // 2
    sent(wide_tiles.at[0:n_y], SEND_Y)
    sent(tiles.at[0:3], SEND_X)
    sent(tiles.at[0:4], SEND_CORE)
    sent(sums_ref.at[1:SECTIONS], SEND_Z)


def finish(entry_count, width, nm_ref, total_ref, sums_ref, nm_out, upd_out, upd, sem):
    stores = [pltpu.make_async_copy(nm_ref, nm_out, sem.at[0])]
    stores[0].start()
    squares = jnp.sum(sums_ref[...], axis=0)
    squares = jnp.sum(jnp.sum(squares, axis=0, keepdims=True), axis=1, keepdims=True)
    scale = lax.rsqrt(squares / entry_count + epsilon)
    for k in range(OWNERS // 2):
        for s in (2 * k, 2 * k + 1):
            upd[:, s * width : (s + 1) * width] = (total_ref[:, s * width : (s + 1) * width] * scale).astype(BF16)
        cols = slice(2 * k * width, 2 * (k + 1) * width)
        stores.append(pltpu.make_async_copy(upd.at[:, cols], upd_out.at[:, cols], sem.at[1 + k]))
        stores[-1].start()
    for copy in stores:
        copy.wait()


def per_device(gradients, momentum, keep_block):
    local_rows, columns = gradients.shape[1:]
    pairs = columns // (OWNERS * LANES)
    width = pairs * LANES
    tables = jnp.asarray(constant_tables())
    col_table = jnp.asarray(column_table())
    entry_count = float(local_rows * lax.axis_size("section") * columns)
    dma = pltpu.SemaphoreType.DMA
    new_momentum, total, sums = pl.pallas_call(
        functools.partial(kernel, pairs),
        out_shape=(
            pltpu.VMEM((local_rows, columns), F32),
            pltpu.VMEM((local_rows, columns), F32),
            pltpu.VMEM((SECTIONS, BLOCK, LANES), F32),
        ),
        in_specs=[pl.BlockSpec(memory_space=pltpu.HBM)] * 5,
        out_specs=(pl.BlockSpec(memory_space=pltpu.VMEM),) * 3,
        scratch_shapes=[
            pltpu.SMEM(keep_block.shape[1:], jnp.int32),
            pltpu.VMEM(keep_block.shape[1:], jnp.int32),
            pltpu.VMEM((local_rows, columns), BF16),
            pltpu.VMEM((local_rows, columns), F32),
            pltpu.VMEM(tables.shape, BF16),
            pltpu.VMEM(col_table.shape, BF16),
            pltpu.VMEM((OWNERS * pairs * BLOCK, LANES), F32),
            pltpu.VMEM((LANES, LANES), BF16),
            pltpu.VMEM((CHIPS_Y, CORES, CHIPS_X, ROWS_SENT, LANES), jnp.int16),
            pltpu.VMEM((CHIPS_Y * CORES * CHIPS_X * ROWS_SENT, LANES), F32),
            pltpu.VMEM((OWNERS * pairs * GROUP, LANES), F32),
            pltpu.VMEM((OWNERS * pairs * 2 * BLOCK, SIDE * GROUP), BF16),
            pltpu.VMEM((OWNERS * pairs * 2 * BLOCK, SIDE * GROUP), BF16),
            pltpu.VMEM((OWNERS * pairs * 2 * BLOCK, 2 * LANES), F32),
            pltpu.VMEM((local_rows, columns), BF16),
            pltpu.VMEM((local_rows, columns), BF16),
            dma((6,)), dma((2,)), dma((4,)), dma((CHIPS_Y,)), dma((CHIPS_Y,)), dma((CHIPS_Y,)), dma,
        ],
        compiler_params=pltpu.CompilerParams(collective_id=0, has_side_effects=True, vmem_limit_bytes=56 << 20),
        name="kept_blocks_step",
    )(keep_block[0], gradients[0], momentum[0], tables, col_table)
    hbm = pl.BlockSpec(memory_space=pltpu.HBM)
    new_momentum, update = pl.pallas_call(
        functools.partial(finish, entry_count, width),
        out_shape=(
            jax.ShapeDtypeStruct((local_rows, columns), F32),
            jax.ShapeDtypeStruct((local_rows, columns), BF16),
        ),
        in_specs=[pl.BlockSpec(memory_space=pltpu.VMEM)] * 3,
        out_specs=(hbm, hbm),
        scratch_shapes=[pltpu.VMEM((local_rows, columns), BF16), dma((1 + OWNERS // 2,))],
        compiler_params=pltpu.CompilerParams(vmem_limit_bytes=32 << 20),
        name="scale_and_store",
    )(new_momentum, total, sums)
    return new_momentum[None], update


def solution(mesh):
    placed = (
        P("replica", "section", None),
        P("replica", "section", None),
        P("replica", "section", None),
    )
    return jax.shard_map(
        per_device,
        mesh=mesh,
        in_specs=placed,
        out_specs=(P("replica", "section", None), P("section", None)),
        check_vma=False,
    )
```

```python
import functools

import jax
import jax.numpy as jnp
import ml_dtypes
import numpy as np
from jax import lax
from jax.experimental import pallas as pl
from jax.experimental.pallas import tpu as pltpu
from jax.sharding import PartitionSpec as P

GROUP = 64
BLOCK = 8
SIDE = GROUP // BLOCK
LANES = 128
CHIPS_X, CHIPS_Y, CORES, SECTIONS = 4, 8, 2, 8
OWNERS = CHIPS_X * CORES
MESH = pl.DeviceIdType.MESH
ROWS_SENT = 48
TOP_BITS = 15
F32, BF16 = jnp.float32, jnp.bfloat16

momentum_decay = 0.9
epsilon = 1e-06


def dct_basis():
    k = np.arange(GROUP, dtype=np.float64)[:, None]
    n = np.arange(GROUP, dtype=np.float64)[None, :]
    basis = np.sqrt(2.0 / GROUP) * np.cos(np.pi * (2.0 * n + 1.0) * k / (2.0 * GROUP))
    basis[0] /= np.sqrt(2.0)
    return basis.astype(np.float32)


def two_terms(values):
    high = values.astype(ml_dtypes.bfloat16)
    low = (values - high.astype(np.float32)).astype(ml_dtypes.bfloat16)
    return high, low


def constant_tables():
    basis = dct_basis()

    def right(matrix):
        high, low = two_terms(np.kron(np.eye(2, dtype=np.float32), matrix))
        return np.concatenate([high, high, low], axis=0)

    def left(matrix):
        high, low = two_terms(matrix)
        wide = np.concatenate([high, high, low, np.zeros_like(low)], axis=1)
        return np.concatenate([wide[:, :LANES], wide[:, LANES:]], axis=0)

    by_row_in_block = np.arange(GROUP).reshape(SIDE, BLOCK).T.reshape(-1)
    return np.concatenate(
        [right(basis.T), right(basis), left(basis), left(basis.T), left(basis.T[:, by_row_in_block])], axis=0
    )


def column_table():
    basis = dct_basis().reshape(SIDE, BLOCK, GROUP)
    table = np.einsum("qmn,ij->qimjn", basis, np.eye(BLOCK, dtype=np.float32))
    terms = np.stack(two_terms(table.reshape(SIDE * GROUP, BLOCK * GROUP)))
    return terms.reshape(2, SIDE * GROUP, BLOCK * GROUP // LANES, LANES).transpose(0, 2, 1, 3).reshape(-1, LANES)


def split(values):
    high = values.astype(BF16)
    low = (values - high.astype(F32)).astype(BF16)
    return high, low


def mm(a, b):
    return jnp.dot(a, b, preferred_element_type=F32)


def kernel(
    pairs, kb_hbm, g_ref, m_ref, tab_ref, col_ref, nm_ref, total_ref, sums_ref,
    kb_ref, kb_row, g_buf, m_buf, tab, col_tab, masked, fold, tiles, wide_tiles, spectra, spec_high, spec_low, wide_cols, total_high, total_low,
    load_sem, kb_sem, send_sem, y_recv, x_recv, core_recv, z_recv,
):
    width = pairs * LANES
    n_blocks = 2 * pairs
    replica, section = lax.axis_index("replica"), lax.axis_index("section")
    x = replica // (CHIPS_Y * CORES)
    y = (replica // CORES) % CHIPS_Y
    core = replica % CORES

    def peer(dx=0, dy=0, dc=0, dz=0):
        px, py, pc = (x + dx) % CHIPS_X, (y + dy) % CHIPS_Y, (core + dc) % CORES
        return ((px * CHIPS_Y + py) * CORES + pc, (section + dz) % SECTIONS)

    n_pairs = OWNERS * pairs
    group_y = sorted(range(1, CHIPS_Y), key=lambda d: -min(d, CHIPS_Y - d))
    group_x = (2, 1, 3)
    row_order = (0, 2, 3, 1, 6, 7, 5, 4)
    grouped = 4

    half = OWNERS // 2 * width
    loads = []
    kb_load = pltpu.make_async_copy(kb_hbm, kb_ref, kb_sem.at[0])
    kb_row_load = pltpu.make_async_copy(kb_hbm, kb_row, kb_sem.at[1])
    tab_load = pltpu.make_async_copy(tab_ref, tab, load_sem.at[4])
    for h in range(2):
        cols = slice(h * half, (h + 1) * half)
        pair = (
            pltpu.make_async_copy(m_ref.at[:, cols], m_buf.at[:, cols], load_sem.at[2 * h]),
            pltpu.make_async_copy(g_ref.at[:, cols], g_buf.at[:, cols], load_sem.at[2 * h + 1]),
        )
        loads.append(pair)
        pair[0].start()
        pair[1].start()
        if h == 0:
            kb_load.start()
            kb_row_load.start()
            tab_load.start()

    col_load = pltpu.make_async_copy(col_ref, col_tab, load_sem.at[5])

    barrier = pltpu.get_barrier_semaphore()
    everyone = (
        [peer(dx=d) for d in group_x]
        + [peer(dy=d) for d in group_y]
        + [peer(dz=d) for d in range(1, SECTIONS)]
        + [peer(dc=1)]
    )
    for other in everyone:
        pl.semaphore_signal(barrier, inc=1, device_id=other, device_id_type=MESH)

    lane8 = lax.broadcasted_iota(jnp.int32, (BLOCK, LANES), 1)
    row8 = lax.broadcasted_iota(jnp.int32, (BLOCK, LANES), 0)
    upper = lane8 >= GROUP
    lane_q = (lane8 % GROUP) // BLOCK
    row_g = lax.broadcasted_iota(jnp.int32, (LANES, LANES), 0)
    lane_g = lax.broadcasted_iota(jnp.int32, (LANES, LANES), 1)
    same_hm = (row_g // GROUP == lane_g // GROUP) & (row_g % BLOCK == lane_g % BLOCK)
    fold[...] = jnp.where(same_hm, 1.0, 0.0).astype(BF16)

    kb_load.wait()
    kb_row_load.wait()
    numbers = jnp.concatenate([kb_row[...].astype(F32), jnp.zeros((1, LANES - kb_row.shape[1]), F32)], axis=1)
    tab_load.wait()
    right_fwd = tab[0:384, :]
    right_inv = tab[384:768, :]
    left_fwd = jnp.concatenate([tab[768:832, :], tab[832:896, 0:64]], axis=1)
    left_inv = jnp.concatenate([tab[896:960, :], tab[960:1024, 0:64]], axis=1)
    left_inv_ip = jnp.concatenate([tab[1024:1088, :], tab[1088:1152, 0:64]], axis=1)

    def block_pair(s, j):
        c = s * n_blocks + 2 * j
        return kb_ref[0, c], kb_ref[0, c + 1]

    def p_lanes(s, j):
        k0, k1 = block_pair(s, j)
        return jnp.where(upper, k1 // SIDE, k0 // SIDE)

    def q_lanes(s, j):
        k0, k1 = block_pair(s, j)
        return jnp.where(upper, k1 % SIDE, k0 % SIDE)

    chosen = []
    for s in range(OWNERS):
        if s % (OWNERS // 2) == 0:
            for copy in loads[s // (OWNERS // 2)]:
                copy.wait()
        cols = slice(s * width, (s + 1) * width)
        moments = momentum_decay * m_buf[:, cols] + g_buf[:, cols].astype(F32)
        nm_ref[:, cols] = moments
        high, low = split(moments)
        rows = mm(left_fwd, jnp.concatenate([high, low, high], axis=0))
        for j in range(pairs):
            p_of = p_lanes(s, j)
            picked = jnp.zeros((BLOCK, LANES), F32)
            for p in range(SIDE):
                picked = jnp.where(p_of == p, rows[p * BLOCK : (p + 1) * BLOCK, j * LANES : (j + 1) * LANES], picked)
            chosen.append(picked)

    col_load.start()

    high, low = split(jnp.concatenate(chosen, axis=0))
    spectrum = mm(jnp.concatenate([high, low, high], axis=1), right_fwd)
    largest = jnp.zeros((BLOCK, LANES), F32)
    for s in range(OWNERS):
        for j in range(pairs):
            row = (s * pairs + j) * BLOCK
            kept = jnp.where(q_lanes(s, j) == lane_q, spectrum[row : row + BLOCK, :], 0.0)
            masked[row : row + BLOCK, :] = kept
            largest = jnp.maximum(largest, jnp.abs(kept))

    kept_high, kept_low = split(masked[...])
    folded = mm(kept_high, fold[...]) + mm(kept_low, fold[...])
    lines = []
    for k in range(n_pairs):
        piece = jnp.where(row8 == lane_q, folded[k * BLOCK : (k + 1) * BLOCK, :], 0.0)
        for shift in (4, 2, 1):
            piece = piece + pltpu.roll(piece, shift, 0)
        if k % BLOCK == 0:
            lines.append(piece)
        else:
            lines[-1] = jnp.where(row8 == k % BLOCK, piece, lines[-1])

    largest = jnp.max(jnp.max(largest, axis=0, keepdims=True), axis=1, keepdims=True)
    exponent = jnp.ceil(jnp.log2(jnp.maximum(largest, 1e-30)) + 0.01)
    to_code = jnp.exp2(TOP_BITS - exponent)
    coded = [jnp.round(line * to_code) for line in lines]
    coded.append(jnp.where(row8 == 0, numbers, jnp.where(row8 == 1, exponent, 0.0)))
    coded = jnp.concatenate(coded, axis=0).astype(jnp.int32).astype(jnp.int16)
    tiles[y, core, 0] = coded

    pl.semaphore_wait(barrier, len(everyone))

    SEND_Y, SEND_X, SEND_CORE, SEND_Z = range(4)

    def remote(src, dst, which, recv, other):
        return pltpu.make_async_remote_copy(
            src_ref=src, dst_ref=dst, send_sem=send_sem.at[which], recv_sem=recv, device_id=other, device_id_type=MESH
        )

    def received(ref, recv):
        remote(ref, ref, SEND_Y, recv, peer(dc=1)).wait_recv()

    def sent(ref, which):
        remote(ref, ref, which, z_recv, peer(dc=1)).wait_send()

    def along_x(row):
        mark = jnp.maximum(row - grouped + 1, 0)
        for d in group_x:
            remote(tiles.at[row, core, 0], tiles.at[row, core, CHIPS_X - d], SEND_X, x_recv.at[mark], peer(dx=d)).start()

    def to_core(rows, mark):
        received(tiles.at[rows, core, 1:CHIPS_X], x_recv.at[mark])
        remote(tiles.at[rows, core], tiles.at[rows, core], SEND_CORE, core_recv.at[mark], peer(dc=1)).start()

    for d in group_y:
        remote(tiles.at[y, core, 0], tiles.at[y, core, 0], SEND_Y, y_recv.at[y], peer(dy=d)).start()
    along_x(y)

    wide = mm(jnp.concatenate([kept_high, kept_low, kept_high], axis=1), right_inv)
    for s in range(OWNERS):
        cols = slice(s * width, (s + 1) * width)
        placed = []
        for j in range(pairs):
            p_of = p_lanes(s, j)
            row = (s * pairs + j) * BLOCK
            piece = wide[row : row + BLOCK, :]
            placed.append(jnp.concatenate([jnp.where(p_of == p, piece, 0.0) for p in range(SIDE)], axis=0))
        high, low = split(jnp.concatenate(placed, axis=1))
        nm_ref[:, cols] = nm_ref[:, cols] - mm(left_inv, jnp.concatenate([high, low, high], axis=0))

    for row in row_order:

        @pl.when(y != row)
        def _():
            received(tiles.at[row, core, 0], y_recv.at[row])
            along_x(row)

    late_rows = row_order[grouped:]
    to_core(slice(0, grouped), 0)
    for row in late_rows:
        to_core(row, row - grouped + 1)
    n_replica = CHIPS_Y * CORES * CHIPS_X
    of_row = CORES * CHIPS_X * ROWS_SENT
    received(tiles.at[0:grouped, 1 - core], core_recv.at[0])
    for row in tuple(range(grouped)) + late_rows:
        if row >= grouped:
            received(tiles.at[row, 1 - core], core_recv.at[row - grouped + 1])
        values = tiles[row].reshape(of_row, LANES).astype(jnp.int32).astype(F32)
        wide_tiles[row * of_row : (row + 1) * of_row, :] = values

    def halves(tiles_of):
        firsts, seconds = [], []
        for even, odd in zip(tiles_of[0::2], tiles_of[1::2]):
            firsts.append(jnp.where(upper, pltpu.roll(odd, GROUP, 1), even))
            seconds.append(jnp.where(upper, odd, pltpu.roll(even, GROUP, 1)))
        return jnp.concatenate([jnp.concatenate(firsts, axis=1), jnp.concatenate(seconds, axis=1)], axis=0)

    def of_all(line):
        return wide_tiles[pl.ds(line, n_replica, stride=ROWS_SENT), :]

    def across(lines, rows):
        return lax.dot_general(rows, lines.astype(BF16), (((1,), (1,)), ((), ())), preferred_element_type=F32)

    row_n = lax.broadcasted_iota(jnp.int32, (n_pairs, LANES), 0)
    lane_n = lax.broadcasted_iota(jnp.int32, (n_pairs, LANES), 1)
    of_numbers = of_all(n_pairs)
    numbers = jnp.concatenate(
        [across(of_numbers, jnp.where(lane_n == 2 * row_n + h, 1.0, 0.0).astype(BF16)) for h in range(2)], axis=1
    )
    exponents = across(of_all(n_pairs + 1), jnp.where(lane8 == 0, 1.0, 0.0).astype(BF16))[0:1, :]
    from_code = jnp.exp2(jnp.concatenate([exponents, exponents], axis=1) - TOP_BITS)
    row_place = lax.broadcasted_iota(jnp.int32, (GROUP, LANES), 0)
    place = ((row_place % BLOCK) * SIDE + row_place // BLOCK).astype(F32)
    lane64 = lax.broadcasted_iota(jnp.int32, (GROUP, LANES), 1)
    of_first = jnp.where(lane64 < GROUP, 1.0, 0.0).astype(BF16)
    of_second = jnp.where(lane64 < GROUP, 0.0, 1.0).astype(BF16)
    squares = jnp.zeros((BLOCK, LANES), F32)
    for k in range(n_pairs):
        high, low = split(of_all(k))
        where_to = jnp.where(numbers[k : k + 1, :] == place, from_code, 0.0).astype(BF16)
        both = mm(
            jnp.concatenate([where_to, where_to], axis=1),
            jnp.concatenate([high * of_first, high * of_second, low * of_first, low * of_second], axis=0),
        )
        spectra[k * GROUP : (k + 1) * GROUP, :] = both
        for q in range(SIDE):
            piece = both[q * BLOCK : (q + 1) * BLOCK, :]
            squares = squares + piece * piece
    sums_ref[0] = squares
    for other in range(SECTIONS):

        @pl.when(section != other)
        def _():
            d = (other - section + SECTIONS) % SECTIONS
            remote(sums_ref.at[0], sums_ref.at[d], SEND_Z, z_recv, (replica, other)).start()

    col_load.wait()
    tall = SIDE * GROUP
    pieces = [col_tab[i * tall : (i + 1) * tall, :] for i in range(2 * BLOCK * GROUP // LANES)]
    col_high = jnp.concatenate(pieces[: len(pieces) // 2], axis=1)
    col_low = jnp.concatenate(pieces[len(pieces) // 2 :], axis=1)
    for k in range(n_pairs):
        by_q = [spectra[k * GROUP + q * BLOCK : k * GROUP + (q + 1) * BLOCK, :] for q in range(SIDE)]
        high, low = split(halves(by_q))
        spec_high[k * 2 * BLOCK : (k + 1) * 2 * BLOCK, :] = high
        spec_low[k * 2 * BLOCK : (k + 1) * 2 * BLOCK, :] = low
    for side in range(2):
        half_cols = slice(side * 2 * LANES, (side + 1) * 2 * LANES)
        wide_cols[...] = (
            mm(spec_high[...], col_high[:, half_cols])
            + mm(spec_low[...], col_high[:, half_cols])
            + mm(spec_high[...], col_low[:, half_cols])
        )
        for k in range(n_pairs):
            by_i = []
            for a in range(2):
                lanes = slice(a * LANES, (a + 1) * LANES)
                first = wide_cols[2 * k * BLOCK : (2 * k + 1) * BLOCK, lanes]
                second = wide_cols[(2 * k + 1) * BLOCK : (2 * k + 2) * BLOCK, lanes]
                by_i.append(jnp.where(upper, pltpu.roll(second, GROUP, 1), first))
                by_i.append(jnp.where(upper, second, pltpu.roll(first, GROUP, 1)))
            high, low = split(jnp.concatenate(by_i, axis=0))
            rows = slice(side * GROUP // 2, (side + 1) * GROUP // 2)
            total_high[rows, k * LANES : (k + 1) * LANES] = high
            total_low[rows, k * LANES : (k + 1) * LANES] = low
    for s in range(OWNERS):
        cols = slice(s * width, (s + 1) * width)
        high, low = total_high[:, cols], total_low[:, cols]
        total_ref[:, cols] = mm(left_inv_ip, jnp.concatenate([high, low, high], axis=0))

    received(sums_ref.at[1:SECTIONS], z_recv)

    n_y = (CHIPS_Y - 1) * ROWS_SENT // 2
    sent(wide_tiles.at[0:n_y], SEND_Y)
    sent(tiles.at[0:3], SEND_X)
    sent(tiles.at[0:4], SEND_CORE)
    sent(sums_ref.at[1:SECTIONS], SEND_Z)


def finish(entry_count, width, nm_ref, total_ref, sums_ref, nm_out, upd_out, upd, sem):
    stores = [pltpu.make_async_copy(nm_ref, nm_out, sem.at[0])]
    stores[0].start()
    squares = jnp.sum(sums_ref[...], axis=0)
    squares = jnp.sum(jnp.sum(squares, axis=0, keepdims=True), axis=1, keepdims=True)
    scale = lax.rsqrt(squares / entry_count + epsilon)
    for k in range(OWNERS // 2):
        for s in (2 * k, 2 * k + 1):
            upd[:, s * width : (s + 1) * width] = (total_ref[:, s * width : (s + 1) * width] * scale).astype(BF16)
        cols = slice(2 * k * width, 2 * (k + 1) * width)
        stores.append(pltpu.make_async_copy(upd.at[:, cols], upd_out.at[:, cols], sem.at[1 + k]))
        stores[-1].start()
    for copy in stores:
        copy.wait()


def per_device(gradients, momentum, keep_block):
    local_rows, columns = gradients.shape[1:]
    pairs = columns // (OWNERS * LANES)
    width = pairs * LANES
    tables = jnp.asarray(constant_tables())
    col_table = jnp.asarray(column_table())
    entry_count = float(local_rows * lax.axis_size("section") * columns)
    dma = pltpu.SemaphoreType.DMA
    new_momentum, total, sums = pl.pallas_call(
        functools.partial(kernel, pairs),
        out_shape=(
            pltpu.VMEM((local_rows, columns), F32),
            pltpu.VMEM((local_rows, columns), F32),
            pltpu.VMEM((SECTIONS, BLOCK, LANES), F32),
        ),
        in_specs=[pl.BlockSpec(memory_space=pltpu.HBM)] * 5,
        out_specs=(pl.BlockSpec(memory_space=pltpu.VMEM),) * 3,
        scratch_shapes=[
            pltpu.SMEM(keep_block.shape[1:], jnp.int32),
            pltpu.VMEM(keep_block.shape[1:], jnp.int32),
            pltpu.VMEM((local_rows, columns), BF16),
            pltpu.VMEM((local_rows, columns), F32),
            pltpu.VMEM(tables.shape, BF16),
            pltpu.VMEM(col_table.shape, BF16),
            pltpu.VMEM((OWNERS * pairs * BLOCK, LANES), F32),
            pltpu.VMEM((LANES, LANES), BF16),
            pltpu.VMEM((CHIPS_Y, CORES, CHIPS_X, ROWS_SENT, LANES), jnp.int16),
            pltpu.VMEM(((CHIPS_Y * CORES * CHIPS_X + 1) * ROWS_SENT, LANES), F32),
            pltpu.VMEM((OWNERS * pairs * GROUP, LANES), F32),
            pltpu.VMEM((OWNERS * pairs * 2 * BLOCK, SIDE * GROUP), BF16),
            pltpu.VMEM((OWNERS * pairs * 2 * BLOCK, SIDE * GROUP), BF16),
            pltpu.VMEM((OWNERS * pairs * 2 * BLOCK, 2 * LANES), F32),
            pltpu.VMEM((local_rows, columns), BF16),
            pltpu.VMEM((local_rows, columns), BF16),
            dma((6,)), dma((2,)), dma((4,)), dma((CHIPS_Y,)), dma((5,)), dma((5,)), dma,
        ],
        compiler_params=pltpu.CompilerParams(collective_id=0, has_side_effects=True, vmem_limit_bytes=56 << 20),
        name="kept_blocks_step",
    )(keep_block[0], gradients[0], momentum[0], tables, col_table)
    hbm = pl.BlockSpec(memory_space=pltpu.HBM)
    new_momentum, update = pl.pallas_call(
        functools.partial(finish, entry_count, width),
        out_shape=(
            jax.ShapeDtypeStruct((local_rows, columns), F32),
            jax.ShapeDtypeStruct((local_rows, columns), BF16),
        ),
        in_specs=[pl.BlockSpec(memory_space=pltpu.VMEM)] * 3,
        out_specs=(hbm, hbm),
        scratch_shapes=[pltpu.VMEM((local_rows, columns), BF16), dma((1 + OWNERS // 2,))],
        compiler_params=pltpu.CompilerParams(vmem_limit_bytes=32 << 20),
        name="scale_and_store",
    )(new_momentum, total, sums)
    return new_momentum[None], update


def solution(mesh):
    placed = (
        P("replica", "section", None),
        P("replica", "section", None),
        P("replica", "section", None),
    )
    return jax.shard_map(
        per_device,
        mesh=mesh,
        in_specs=placed,
        out_specs=(P("replica", "section", None), P("section", None)),
        check_vma=False,
    )
```

```python
import functools

import jax
import jax.numpy as jnp
import ml_dtypes
import numpy as np
from jax import lax
from jax.experimental import pallas as pl
from jax.experimental.pallas import tpu as pltpu
from jax.sharding import PartitionSpec as P

GROUP = 64
BLOCK = 8
SIDE = GROUP // BLOCK
LANES = 128
CHIPS_X, CHIPS_Y, CORES, SECTIONS = 4, 8, 2, 8
OWNERS = CHIPS_X * CORES
MESH = pl.DeviceIdType.MESH
ROWS_SENT = 48
TOP_BITS = 15
F32, BF16 = jnp.float32, jnp.bfloat16

momentum_decay = 0.9
epsilon = 1e-06


def dct_basis():
    k = np.arange(GROUP, dtype=np.float64)[:, None]
    n = np.arange(GROUP, dtype=np.float64)[None, :]
    basis = np.sqrt(2.0 / GROUP) * np.cos(np.pi * (2.0 * n + 1.0) * k / (2.0 * GROUP))
    basis[0] /= np.sqrt(2.0)
    return basis.astype(np.float32)


def two_terms(values):
    high = values.astype(ml_dtypes.bfloat16)
    low = (values - high.astype(np.float32)).astype(ml_dtypes.bfloat16)
    return high, low


def constant_tables():
    basis = dct_basis()

    def right(matrix):
        high, low = two_terms(np.kron(np.eye(2, dtype=np.float32), matrix))
        return np.concatenate([high, high, low], axis=0)

    def left(matrix):
        high, low = two_terms(matrix)
        wide = np.concatenate([high, high, low, np.zeros_like(low)], axis=1)
        return np.concatenate([wide[:, :LANES], wide[:, LANES:]], axis=0)

    by_row_in_block = np.arange(GROUP).reshape(SIDE, BLOCK).T.reshape(-1)
    return np.concatenate(
        [right(basis.T), right(basis), left(basis), left(basis.T), left(basis.T[:, by_row_in_block])], axis=0
    )


def column_table():
    basis = dct_basis().reshape(SIDE, BLOCK, GROUP)
    table = np.einsum("qmn,ij->qimjn", basis, np.eye(BLOCK, dtype=np.float32))
    terms = np.stack(two_terms(table.reshape(SIDE * GROUP, BLOCK * GROUP)))
    return terms.reshape(2, SIDE * GROUP, BLOCK * GROUP // LANES, LANES).transpose(0, 2, 1, 3).reshape(-1, LANES)


def split(values):
    high = values.astype(BF16)
    low = (values - high.astype(F32)).astype(BF16)
    return high, low


def mm(a, b):
    return jnp.dot(a, b, preferred_element_type=F32)


def kernel(
    pairs, kb_hbm, g_ref, m_ref, tab_ref, col_ref, nm_ref, total_ref, sums_ref,
    kb_ref, kb_row, g_buf, m_buf, tab, col_tab, masked, fold, tiles, wide_tiles, spectra, spec_high, spec_low, wide_cols, total_high, total_low,
    load_sem, kb_sem, send_sem, y_recv, x_recv, core_recv, z_recv,
):
    width = pairs * LANES
    n_blocks = 2 * pairs
    replica, section = lax.axis_index("replica"), lax.axis_index("section")
    x = replica // (CHIPS_Y * CORES)
    y = (replica // CORES) % CHIPS_Y
    core = replica % CORES

    def peer(dx=0, dy=0, dc=0, dz=0):
        px, py, pc = (x + dx) % CHIPS_X, (y + dy) % CHIPS_Y, (core + dc) % CORES
        return ((px * CHIPS_Y + py) * CORES + pc, (section + dz) % SECTIONS)

    n_pairs = OWNERS * pairs
    group_y = sorted(range(1, CHIPS_Y), key=lambda d: -min(d, CHIPS_Y - d))
    group_x = (2, 1, 3)
    row_order = (0, 2, 3, 1, 6, 7, 5, 4)
    direct = (4, 5)
    grouped = 4

    half = OWNERS // 2 * width
    loads = []
    kb_load = pltpu.make_async_copy(kb_hbm, kb_ref, kb_sem.at[0])
    kb_row_load = pltpu.make_async_copy(kb_hbm, kb_row, kb_sem.at[1])
    tab_load = pltpu.make_async_copy(tab_ref, tab, load_sem.at[4])
    for h in range(2):
        cols = slice(h * half, (h + 1) * half)
        pair = (
            pltpu.make_async_copy(m_ref.at[:, cols], m_buf.at[:, cols], load_sem.at[2 * h]),
            pltpu.make_async_copy(g_ref.at[:, cols], g_buf.at[:, cols], load_sem.at[2 * h + 1]),
        )
        loads.append(pair)
        pair[0].start()
        pair[1].start()
        if h == 0:
            kb_load.start()
            kb_row_load.start()
            tab_load.start()

    col_load = pltpu.make_async_copy(col_ref, col_tab, load_sem.at[5])

    barrier = pltpu.get_barrier_semaphore()
    everyone = (
        [peer(dx=d) for d in group_x]
        + [peer(dy=d) for d in group_y]
        + [peer(dz=d) for d in range(1, SECTIONS)]
        + [peer(dc=1)]
        + [peer(dx=d, dc=1) for d in group_x]
    )
    for other in everyone:
        pl.semaphore_signal(barrier, inc=1, device_id=other, device_id_type=MESH)

    lane8 = lax.broadcasted_iota(jnp.int32, (BLOCK, LANES), 1)
    row8 = lax.broadcasted_iota(jnp.int32, (BLOCK, LANES), 0)
    upper = lane8 >= GROUP
    lane_q = (lane8 % GROUP) // BLOCK
    row_g = lax.broadcasted_iota(jnp.int32, (LANES, LANES), 0)
    lane_g = lax.broadcasted_iota(jnp.int32, (LANES, LANES), 1)
    same_hm = (row_g // GROUP == lane_g // GROUP) & (row_g % BLOCK == lane_g % BLOCK)
    fold[...] = jnp.where(same_hm, 1.0, 0.0).astype(BF16)

    kb_load.wait()
    kb_row_load.wait()
    numbers = jnp.concatenate([kb_row[...].astype(F32), jnp.zeros((1, LANES - kb_row.shape[1]), F32)], axis=1)
    tab_load.wait()
    right_fwd = tab[0:384, :]
    right_inv = tab[384:768, :]
    left_fwd = jnp.concatenate([tab[768:832, :], tab[832:896, 0:64]], axis=1)
    left_inv = jnp.concatenate([tab[896:960, :], tab[960:1024, 0:64]], axis=1)
    left_inv_ip = jnp.concatenate([tab[1024:1088, :], tab[1088:1152, 0:64]], axis=1)

    def block_pair(s, j):
        c = s * n_blocks + 2 * j
        return kb_ref[0, c], kb_ref[0, c + 1]

    def p_lanes(s, j):
        k0, k1 = block_pair(s, j)
        return jnp.where(upper, k1 // SIDE, k0 // SIDE)

    def q_lanes(s, j):
        k0, k1 = block_pair(s, j)
        return jnp.where(upper, k1 % SIDE, k0 % SIDE)

    chosen = []
    for s in range(OWNERS):
        if s % (OWNERS // 2) == 0:
            for copy in loads[s // (OWNERS // 2)]:
                copy.wait()
        cols = slice(s * width, (s + 1) * width)
        moments = momentum_decay * m_buf[:, cols] + g_buf[:, cols].astype(F32)
        nm_ref[:, cols] = moments
        high, low = split(moments)
        rows = mm(left_fwd, jnp.concatenate([high, low, high], axis=0))
        for j in range(pairs):
            p_of = p_lanes(s, j)
            picked = jnp.zeros((BLOCK, LANES), F32)
            for p in range(SIDE):
                picked = jnp.where(p_of == p, rows[p * BLOCK : (p + 1) * BLOCK, j * LANES : (j + 1) * LANES], picked)
            chosen.append(picked)

    col_load.start()

    high, low = split(jnp.concatenate(chosen, axis=0))
    spectrum = mm(jnp.concatenate([high, low, high], axis=1), right_fwd)
    largest = jnp.zeros((BLOCK, LANES), F32)
    for s in range(OWNERS):
        for j in range(pairs):
            row = (s * pairs + j) * BLOCK
            kept = jnp.where(q_lanes(s, j) == lane_q, spectrum[row : row + BLOCK, :], 0.0)
            masked[row : row + BLOCK, :] = kept
            largest = jnp.maximum(largest, jnp.abs(kept))

    kept_high, kept_low = split(masked[...])
    folded = mm(kept_high, fold[...]) + mm(kept_low, fold[...])
    lines = []
    for k in range(n_pairs):
        piece = jnp.where(row8 == lane_q, folded[k * BLOCK : (k + 1) * BLOCK, :], 0.0)
        for shift in (4, 2, 1):
            piece = piece + pltpu.roll(piece, shift, 0)
        if k % BLOCK == 0:
            lines.append(piece)
        else:
            lines[-1] = jnp.where(row8 == k % BLOCK, piece, lines[-1])

    largest = jnp.max(jnp.max(largest, axis=0, keepdims=True), axis=1, keepdims=True)
    exponent = jnp.ceil(jnp.log2(jnp.maximum(largest, 1e-30)) + 0.01)
    to_code = jnp.exp2(TOP_BITS - exponent)
    coded = [jnp.round(line * to_code) for line in lines]
    coded.append(jnp.where(row8 == 0, numbers, jnp.where(row8 == 1, exponent, 0.0)))
    coded = jnp.concatenate(coded, axis=0).astype(jnp.int32).astype(jnp.int16)
    tiles[y, core, 0] = coded

    pl.semaphore_wait(barrier, len(everyone))

    SEND_Y, SEND_X, SEND_CORE, SEND_Z = range(4)

    def remote(src, dst, which, recv, other):
        return pltpu.make_async_remote_copy(
            src_ref=src, dst_ref=dst, send_sem=send_sem.at[which], recv_sem=recv, device_id=other, device_id_type=MESH
        )

    def received(ref, recv):
        remote(ref, ref, SEND_Y, recv, peer(dc=1)).wait_recv()

    def sent(ref, which):
        remote(ref, ref, which, z_recv, peer(dc=1)).wait_send()

    def along_x(row):
        mark = jnp.maximum(row - grouped + 1, 0)
        for d in group_x:
            there = tiles.at[row, core, CHIPS_X - d]
            remote(tiles.at[row, core, 0], there, SEND_X, x_recv.at[mark], peer(dx=d)).start()

        def to_both():
            for d in group_x:
                there = tiles.at[row, core, CHIPS_X - d]
                remote(tiles.at[row, core, 0], there, SEND_CORE, core_recv.at[mark], peer(dx=d, dc=1)).start()
            remote(tiles.at[row, core, 0], tiles.at[row, core, 0], SEND_CORE, core_recv.at[mark], peer(dc=1)).start()

        if isinstance(row, int):
            if row in direct:
                to_both()
        else:
            pl.when(sum((row == r).astype(jnp.int32) for r in direct) > 0)(to_both)

    def to_core(rows, mark):
        received(tiles.at[rows, core, 1:CHIPS_X], x_recv.at[mark])
        if rows not in direct:
            remote(tiles.at[rows, core], tiles.at[rows, core], SEND_CORE, core_recv.at[mark], peer(dc=1)).start()

    for d in group_y:
        remote(tiles.at[y, core, 0], tiles.at[y, core, 0], SEND_Y, y_recv.at[y], peer(dy=d)).start()
    along_x(y)

    wide = mm(jnp.concatenate([kept_high, kept_low, kept_high], axis=1), right_inv)
    for s in range(OWNERS):
        cols = slice(s * width, (s + 1) * width)
        placed = []
        for j in range(pairs):
            p_of = p_lanes(s, j)
            row = (s * pairs + j) * BLOCK
            piece = wide[row : row + BLOCK, :]
            placed.append(jnp.concatenate([jnp.where(p_of == p, piece, 0.0) for p in range(SIDE)], axis=0))
        high, low = split(jnp.concatenate(placed, axis=1))
        nm_ref[:, cols] = nm_ref[:, cols] - mm(left_inv, jnp.concatenate([high, low, high], axis=0))

    for row in row_order:

        @pl.when(y != row)
        def _():
            received(tiles.at[row, core, 0], y_recv.at[row])
            along_x(row)

    late_rows = row_order[grouped:]
    to_core(slice(0, grouped), 0)
    for row in late_rows:
        to_core(row, row - grouped + 1)
    n_replica = CHIPS_Y * CORES * CHIPS_X
    of_row = CORES * CHIPS_X * ROWS_SENT
    received(tiles.at[0:grouped, 1 - core], core_recv.at[0])
    for row in tuple(range(grouped)) + late_rows:
        if row >= grouped:
            received(tiles.at[row, 1 - core], core_recv.at[row - grouped + 1])
        values = tiles[row].reshape(of_row, LANES).astype(jnp.int32).astype(F32)
        wide_tiles[row * of_row : (row + 1) * of_row, :] = values

    def halves(tiles_of):
        firsts, seconds = [], []
        for even, odd in zip(tiles_of[0::2], tiles_of[1::2]):
            firsts.append(jnp.where(upper, pltpu.roll(odd, GROUP, 1), even))
            seconds.append(jnp.where(upper, odd, pltpu.roll(even, GROUP, 1)))
        return jnp.concatenate([jnp.concatenate(firsts, axis=1), jnp.concatenate(seconds, axis=1)], axis=0)

    def of_all(line):
        return wide_tiles[pl.ds(line, n_replica, stride=ROWS_SENT), :]

    def across(lines, rows):
        return lax.dot_general(rows, lines.astype(BF16), (((1,), (1,)), ((), ())), preferred_element_type=F32)

    row_n = lax.broadcasted_iota(jnp.int32, (n_pairs, LANES), 0)
    lane_n = lax.broadcasted_iota(jnp.int32, (n_pairs, LANES), 1)
    of_numbers = of_all(n_pairs)
    numbers = jnp.concatenate(
        [across(of_numbers, jnp.where(lane_n == 2 * row_n + h, 1.0, 0.0).astype(BF16)) for h in range(2)], axis=1
    )
    exponents = across(of_all(n_pairs + 1), jnp.where(lane8 == 0, 1.0, 0.0).astype(BF16))[0:1, :]
    from_code = jnp.exp2(jnp.concatenate([exponents, exponents], axis=1) - TOP_BITS)
    row_place = lax.broadcasted_iota(jnp.int32, (GROUP, LANES), 0)
    place = ((row_place % BLOCK) * SIDE + row_place // BLOCK).astype(F32)
    lane64 = lax.broadcasted_iota(jnp.int32, (GROUP, LANES), 1)
    of_first = jnp.where(lane64 < GROUP, 1.0, 0.0).astype(BF16)
    of_second = jnp.where(lane64 < GROUP, 0.0, 1.0).astype(BF16)
    squares = jnp.zeros((BLOCK, LANES), F32)
    for k in range(n_pairs):
        high, low = split(of_all(k))
        where_to = jnp.where(numbers[k : k + 1, :] == place, from_code, 0.0).astype(BF16)
        both = mm(
            jnp.concatenate([where_to, where_to], axis=1),
            jnp.concatenate([high * of_first, high * of_second, low * of_first, low * of_second], axis=0),
        )
        spectra[k * GROUP : (k + 1) * GROUP, :] = both
        for q in range(SIDE):
            piece = both[q * BLOCK : (q + 1) * BLOCK, :]
            squares = squares + piece * piece
    sums_ref[0] = squares
    for other in range(SECTIONS):

        @pl.when(section != other)
        def _():
            d = (other - section + SECTIONS) % SECTIONS
            remote(sums_ref.at[0], sums_ref.at[d], SEND_Z, z_recv, (replica, other)).start()

    col_load.wait()
    tall = SIDE * GROUP
    pieces = [col_tab[i * tall : (i + 1) * tall, :] for i in range(2 * BLOCK * GROUP // LANES)]
    col_high = jnp.concatenate(pieces[: len(pieces) // 2], axis=1)
    col_low = jnp.concatenate(pieces[len(pieces) // 2 :], axis=1)
    for k in range(n_pairs):
        by_q = [spectra[k * GROUP + q * BLOCK : k * GROUP + (q + 1) * BLOCK, :] for q in range(SIDE)]
        high, low = split(halves(by_q))
        spec_high[k * 2 * BLOCK : (k + 1) * 2 * BLOCK, :] = high
        spec_low[k * 2 * BLOCK : (k + 1) * 2 * BLOCK, :] = low
    for side in range(2):
        half_cols = slice(side * 2 * LANES, (side + 1) * 2 * LANES)
        wide_cols[...] = (
            mm(spec_high[...], col_high[:, half_cols])
            + mm(spec_low[...], col_high[:, half_cols])
            + mm(spec_high[...], col_low[:, half_cols])
        )
        for k in range(n_pairs):
            by_i = []
            for a in range(2):
                lanes = slice(a * LANES, (a + 1) * LANES)
                first = wide_cols[2 * k * BLOCK : (2 * k + 1) * BLOCK, lanes]
                second = wide_cols[(2 * k + 1) * BLOCK : (2 * k + 2) * BLOCK, lanes]
                by_i.append(jnp.where(upper, pltpu.roll(second, GROUP, 1), first))
                by_i.append(jnp.where(upper, second, pltpu.roll(first, GROUP, 1)))
            high, low = split(jnp.concatenate(by_i, axis=0))
            rows = slice(side * GROUP // 2, (side + 1) * GROUP // 2)
            total_high[rows, k * LANES : (k + 1) * LANES] = high
            total_low[rows, k * LANES : (k + 1) * LANES] = low
    for s in range(OWNERS):
        cols = slice(s * width, (s + 1) * width)
        high, low = total_high[:, cols], total_low[:, cols]
        total_ref[:, cols] = mm(left_inv_ip, jnp.concatenate([high, low, high], axis=0))

    received(sums_ref.at[1:SECTIONS], z_recv)

    n_y = (CHIPS_Y - 1) * ROWS_SENT // 2
    sent(wide_tiles.at[0:n_y], SEND_Y)
    sent(tiles.at[0:3], SEND_X)
    sent(tiles.at[0:4], SEND_CORE)
    sent(sums_ref.at[1:SECTIONS], SEND_Z)


def finish(entry_count, width, nm_ref, total_ref, sums_ref, nm_out, upd_out, upd, sem):
    stores = [pltpu.make_async_copy(nm_ref, nm_out, sem.at[0])]
    stores[0].start()
    squares = jnp.sum(sums_ref[...], axis=0)
    squares = jnp.sum(jnp.sum(squares, axis=0, keepdims=True), axis=1, keepdims=True)
    scale = lax.rsqrt(squares / entry_count + epsilon)
    for k in range(OWNERS // 2):
        for s in (2 * k, 2 * k + 1):
            upd[:, s * width : (s + 1) * width] = (total_ref[:, s * width : (s + 1) * width] * scale).astype(BF16)
        cols = slice(2 * k * width, 2 * (k + 1) * width)
        stores.append(pltpu.make_async_copy(upd.at[:, cols], upd_out.at[:, cols], sem.at[1 + k]))
        stores[-1].start()
    for copy in stores:
        copy.wait()


def per_device(gradients, momentum, keep_block):
    local_rows, columns = gradients.shape[1:]
    pairs = columns // (OWNERS * LANES)
    width = pairs * LANES
    tables = jnp.asarray(constant_tables())
    col_table = jnp.asarray(column_table())
    entry_count = float(local_rows * lax.axis_size("section") * columns)
    dma = pltpu.SemaphoreType.DMA
    new_momentum, total, sums = pl.pallas_call(
        functools.partial(kernel, pairs),
        out_shape=(
            pltpu.VMEM((local_rows, columns), F32),
            pltpu.VMEM((local_rows, columns), F32),
            pltpu.VMEM((SECTIONS, BLOCK, LANES), F32),
        ),
        in_specs=[pl.BlockSpec(memory_space=pltpu.HBM)] * 5,
        out_specs=(pl.BlockSpec(memory_space=pltpu.VMEM),) * 3,
        scratch_shapes=[
            pltpu.SMEM(keep_block.shape[1:], jnp.int32),
            pltpu.VMEM(keep_block.shape[1:], jnp.int32),
            pltpu.VMEM((local_rows, columns), BF16),
            pltpu.VMEM((local_rows, columns), F32),
            pltpu.VMEM(tables.shape, BF16),
            pltpu.VMEM(col_table.shape, BF16),
            pltpu.VMEM((OWNERS * pairs * BLOCK, LANES), F32),
            pltpu.VMEM((LANES, LANES), BF16),
            pltpu.VMEM((CHIPS_Y, CORES, CHIPS_X, ROWS_SENT, LANES), jnp.int16),
            pltpu.VMEM(((CHIPS_Y * CORES * CHIPS_X + 1) * ROWS_SENT, LANES), F32),
            pltpu.VMEM((OWNERS * pairs * GROUP, LANES), F32),
            pltpu.VMEM((OWNERS * pairs * 2 * BLOCK, SIDE * GROUP), BF16),
            pltpu.VMEM((OWNERS * pairs * 2 * BLOCK, SIDE * GROUP), BF16),
            pltpu.VMEM((OWNERS * pairs * 2 * BLOCK, 2 * LANES), F32),
            pltpu.VMEM((local_rows, columns), BF16),
            pltpu.VMEM((local_rows, columns), BF16),
            dma((6,)), dma((2,)), dma((4,)), dma((CHIPS_Y,)), dma((5,)), dma((5,)), dma,
        ],
        compiler_params=pltpu.CompilerParams(collective_id=0, has_side_effects=True, vmem_limit_bytes=56 << 20),
        name="kept_blocks_step",
    )(keep_block[0], gradients[0], momentum[0], tables, col_table)
    hbm = pl.BlockSpec(memory_space=pltpu.HBM)
    new_momentum, update = pl.pallas_call(
        functools.partial(finish, entry_count, width),
        out_shape=(
            jax.ShapeDtypeStruct((local_rows, columns), F32),
            jax.ShapeDtypeStruct((local_rows, columns), BF16),
        ),
        in_specs=[pl.BlockSpec(memory_space=pltpu.VMEM)] * 3,
        out_specs=(hbm, hbm),
        scratch_shapes=[pltpu.VMEM((local_rows, columns), BF16), dma((1 + OWNERS // 2,))],
        compiler_params=pltpu.CompilerParams(vmem_limit_bytes=32 << 20),
        name="scale_and_store",
    )(new_momentum, total, sums)
    return new_momentum[None], update


def solution(mesh):
    placed = (
        P("replica", "section", None),
        P("replica", "section", None),
        P("replica", "section", None),
    )
    return jax.shard_map(
        per_device,
        mesh=mesh,
        in_specs=placed,
        out_specs=(P("replica", "section", None), P("section", None)),
        check_vma=False,
    )
```

```python
import functools

import jax
import jax.numpy as jnp
import ml_dtypes
import numpy as np
from jax import lax
from jax.experimental import pallas as pl
from jax.experimental.pallas import tpu as pltpu
from jax.sharding import PartitionSpec as P

GROUP = 64
BLOCK = 8
SIDE = GROUP // BLOCK
LANES = 128
CHIPS_X, CHIPS_Y, CORES, SECTIONS = 4, 8, 2, 8
OWNERS = CHIPS_X * CORES
MESH = pl.DeviceIdType.MESH
ROWS_SENT = 48
TOP_BITS = 15
F32, BF16 = jnp.float32, jnp.bfloat16

momentum_decay = 0.9
epsilon = 1e-06


def dct_basis():
    k = np.arange(GROUP, dtype=np.float64)[:, None]
    n = np.arange(GROUP, dtype=np.float64)[None, :]
    basis = np.sqrt(2.0 / GROUP) * np.cos(np.pi * (2.0 * n + 1.0) * k / (2.0 * GROUP))
    basis[0] /= np.sqrt(2.0)
    return basis.astype(np.float32)


def two_terms(values):
    high = values.astype(ml_dtypes.bfloat16)
    low = (values - high.astype(np.float32)).astype(ml_dtypes.bfloat16)
    return high, low


def constant_tables():
    basis = dct_basis()

    def right(matrix):
        high, low = two_terms(np.kron(np.eye(2, dtype=np.float32), matrix))
        return np.concatenate([high, high, low], axis=0)

    def left(matrix):
        high, low = two_terms(matrix)
        wide = np.concatenate([high, high, low, np.zeros_like(low)], axis=1)
        return np.concatenate([wide[:, :LANES], wide[:, LANES:]], axis=0)

    by_row_in_block = np.arange(GROUP).reshape(SIDE, BLOCK).T.reshape(-1)
    return np.concatenate(
        [right(basis.T), right(basis), left(basis), left(basis.T), left(basis.T[:, by_row_in_block])], axis=0
    )


def column_table():
    basis = dct_basis().reshape(SIDE, BLOCK, GROUP)
    table = np.einsum("qmn,ij->qimjn", basis, np.eye(BLOCK, dtype=np.float32))
    terms = np.stack(two_terms(table.reshape(SIDE * GROUP, BLOCK * GROUP)))
    return terms.reshape(2, SIDE * GROUP, BLOCK * GROUP // LANES, LANES).transpose(0, 2, 1, 3).reshape(-1, LANES)


def split(values):
    high = values.astype(BF16)
    low = (values - high.astype(F32)).astype(BF16)
    return high, low


def mm(a, b):
    return jnp.dot(a, b, preferred_element_type=F32)


def kernel(
    pairs, kb_hbm, g_ref, m_ref, tab_ref, col_ref, nm_ref, total_ref, sums_ref,
    kb_ref, kb_row, g_buf, m_buf, tab, col_tab, masked, fold, tiles, wide_tiles, spectra, spec_high, spec_low, wide_cols, total_high, total_low,
    load_sem, kb_sem, send_sem, y_recv, x_recv, core_recv, z_recv,
):
    width = pairs * LANES
    n_blocks = 2 * pairs
    replica, section = lax.axis_index("replica"), lax.axis_index("section")
    x = replica // (CHIPS_Y * CORES)
    y = (replica // CORES) % CHIPS_Y
    core = replica % CORES

    def peer(dx=0, dy=0, dc=0, dz=0):
        px, py, pc = (x + dx) % CHIPS_X, (y + dy) % CHIPS_Y, (core + dc) % CORES
        return ((px * CHIPS_Y + py) * CORES + pc, (section + dz) % SECTIONS)

    n_pairs = OWNERS * pairs
    group_y = sorted(range(1, CHIPS_Y), key=lambda d: -min(d, CHIPS_Y - d))
    group_x = (2, 1, 3)
    row_order = (0, 2, 3, 1, 6, 7, 5, 4)
    direct = (4, 5)
    grouped = 4

    half = OWNERS // 2 * width
    loads = []
    kb_load = pltpu.make_async_copy(kb_hbm, kb_ref, kb_sem.at[0])
    kb_row_load = pltpu.make_async_copy(kb_hbm, kb_row, kb_sem.at[1])
    tab_load = pltpu.make_async_copy(tab_ref, tab, load_sem.at[4])
    for h in range(2):
        cols = slice(h * half, (h + 1) * half)
        pair = (
            pltpu.make_async_copy(m_ref.at[:, cols], m_buf.at[:, cols], load_sem.at[2 * h]),
            pltpu.make_async_copy(g_ref.at[:, cols], g_buf.at[:, cols], load_sem.at[2 * h + 1]),
        )
        loads.append(pair)
        pair[0].start()
        pair[1].start()
        if h == 0:
            kb_load.start()
            kb_row_load.start()
            tab_load.start()

    col_load = pltpu.make_async_copy(col_ref, col_tab, load_sem.at[5])

    barrier = pltpu.get_barrier_semaphore()
    everyone = (
        [peer(dx=d) for d in group_x]
        + [peer(dy=d) for d in group_y]
        + [peer(dz=d) for d in range(1, SECTIONS)]
        + [peer(dc=1)]
        + [peer(dx=d, dc=1) for d in group_x]
    )
    for other in everyone:
        pl.semaphore_signal(barrier, inc=1, device_id=other, device_id_type=MESH)

    lane8 = lax.broadcasted_iota(jnp.int32, (BLOCK, LANES), 1)
    row8 = lax.broadcasted_iota(jnp.int32, (BLOCK, LANES), 0)
    upper = lane8 >= GROUP
    lane_q = (lane8 % GROUP) // BLOCK
    row_g = lax.broadcasted_iota(jnp.int32, (LANES, LANES), 0)
    lane_g = lax.broadcasted_iota(jnp.int32, (LANES, LANES), 1)
    same_hm = (row_g // GROUP == lane_g // GROUP) & (row_g % BLOCK == lane_g % BLOCK)
    fold[...] = jnp.where(same_hm, 1.0, 0.0).astype(BF16)

    kb_load.wait()
    kb_row_load.wait()
    numbers = jnp.concatenate([kb_row[...].astype(F32), jnp.zeros((1, LANES - kb_row.shape[1]), F32)], axis=1)
    tab_load.wait()
    right_fwd = tab[0:384, :]
    right_inv = tab[384:768, :]
    left_fwd = jnp.concatenate([tab[768:832, :], tab[832:896, 0:64]], axis=1)
    left_inv = jnp.concatenate([tab[896:960, :], tab[960:1024, 0:64]], axis=1)
    left_inv_ip = jnp.concatenate([tab[1024:1088, :], tab[1088:1152, 0:64]], axis=1)

    def block_pair(s, j):
        c = s * n_blocks + 2 * j
        return kb_ref[0, c], kb_ref[0, c + 1]

    def p_lanes(s, j):
        k0, k1 = block_pair(s, j)
        return jnp.where(upper, k1 // SIDE, k0 // SIDE)

    def q_lanes(s, j):
        k0, k1 = block_pair(s, j)
        return jnp.where(upper, k1 % SIDE, k0 % SIDE)

    chosen = []
    for s in range(OWNERS):
        if s % (OWNERS // 2) == 0:
            for copy in loads[s // (OWNERS // 2)]:
                copy.wait()
        cols = slice(s * width, (s + 1) * width)
        moments = momentum_decay * m_buf[:, cols] + g_buf[:, cols].astype(F32)
        nm_ref[:, cols] = moments
        high, low = split(moments)
        rows = mm(left_fwd, jnp.concatenate([high, low, high], axis=0))
        for j in range(pairs):
            p_of = p_lanes(s, j)
            picked = jnp.zeros((BLOCK, LANES), F32)
            for p in range(SIDE):
                picked = jnp.where(p_of == p, rows[p * BLOCK : (p + 1) * BLOCK, j * LANES : (j + 1) * LANES], picked)
            chosen.append(picked)

    col_load.start()

    high, low = split(jnp.concatenate(chosen, axis=0))
    spectrum = mm(jnp.concatenate([high, low, high], axis=1), right_fwd)
    largest = jnp.zeros((BLOCK, LANES), F32)
    for s in range(OWNERS):
        for j in range(pairs):
            row = (s * pairs + j) * BLOCK
            kept = jnp.where(q_lanes(s, j) == lane_q, spectrum[row : row + BLOCK, :], 0.0)
            masked[row : row + BLOCK, :] = kept
            largest = jnp.maximum(largest, jnp.abs(kept))

    kept_high, kept_low = split(masked[...])
    folded = mm(kept_high, fold[...]) + mm(kept_low, fold[...])
    lines = []
    for k in range(n_pairs):
        piece = jnp.where(row8 == lane_q, folded[k * BLOCK : (k + 1) * BLOCK, :], 0.0)
        for shift in (4, 2, 1):
            piece = piece + pltpu.roll(piece, shift, 0)
        if k % BLOCK == 0:
            lines.append(piece)
        else:
            lines[-1] = jnp.where(row8 == k % BLOCK, piece, lines[-1])

    largest = jnp.max(jnp.max(largest, axis=0, keepdims=True), axis=1, keepdims=True)
    exponent = jnp.ceil(jnp.log2(jnp.maximum(largest, 1e-30)) + 0.01)
    to_code = jnp.exp2(TOP_BITS - exponent)
    coded = [jnp.round(line * to_code) for line in lines]
    coded.append(jnp.where(row8 == 0, numbers, jnp.where(row8 == 1, exponent, 0.0)))
    coded = jnp.concatenate(coded, axis=0).astype(jnp.int32).astype(jnp.int16)
    tiles[y, core, 0] = coded

    pl.semaphore_wait(barrier, len(everyone))

    SEND_Y, SEND_X, SEND_CORE, SEND_Z = range(4)

    def remote(src, dst, which, recv, other):
        return pltpu.make_async_remote_copy(
            src_ref=src, dst_ref=dst, send_sem=send_sem.at[which], recv_sem=recv, device_id=other, device_id_type=MESH
        )

    def received(ref, recv):
        remote(ref, ref, SEND_Y, recv, peer(dc=1)).wait_recv()

    def sent(ref, which):
        remote(ref, ref, which, z_recv, peer(dc=1)).wait_send()

    def along_x(row):
        mark = jnp.maximum(row - grouped + 1, 0)

        def to_same(d):
            there = tiles.at[row, core, CHIPS_X - d]
            remote(tiles.at[row, core, 0], there, SEND_X, x_recv.at[mark], peer(dx=d)).start()

        def to_other(d):
            there = tiles.at[row, core, CHIPS_X - d]
            remote(tiles.at[row, core, 0], there, SEND_CORE, core_recv.at[mark], peer(dx=d, dc=1)).start()

        def to_partner():
            remote(tiles.at[row, core, 0], tiles.at[row, core, 0], SEND_CORE, core_recv.at[mark], peer(dc=1)).start()

        if isinstance(row, int) and row in direct:
            for d in group_x:
                to_other(d)
                to_same(d)
            to_partner()
            return
        for d in group_x:
            to_same(d)
        if not isinstance(row, int):

            @pl.when(sum((row == r).astype(jnp.int32) for r in direct) > 0)
            def _():
                for d in group_x:
                    to_other(d)
                to_partner()

    def to_core(rows, mark):
        received(tiles.at[rows, core, 1:CHIPS_X], x_recv.at[mark])
        if rows not in direct:
            remote(tiles.at[rows, core], tiles.at[rows, core], SEND_CORE, core_recv.at[mark], peer(dc=1)).start()

    for d in group_y:
        remote(tiles.at[y, core, 0], tiles.at[y, core, 0], SEND_Y, y_recv.at[y], peer(dy=d)).start()
    along_x(y)

    wide = mm(jnp.concatenate([kept_high, kept_low, kept_high], axis=1), right_inv)
    for s in range(OWNERS):
        cols = slice(s * width, (s + 1) * width)
        placed = []
        for j in range(pairs):
            p_of = p_lanes(s, j)
            row = (s * pairs + j) * BLOCK
            piece = wide[row : row + BLOCK, :]
            placed.append(jnp.concatenate([jnp.where(p_of == p, piece, 0.0) for p in range(SIDE)], axis=0))
        high, low = split(jnp.concatenate(placed, axis=1))
        nm_ref[:, cols] = nm_ref[:, cols] - mm(left_inv, jnp.concatenate([high, low, high], axis=0))

    for row in row_order:

        @pl.when(y != row)
        def _():
            received(tiles.at[row, core, 0], y_recv.at[row])
            along_x(row)

    late_rows = row_order[grouped:]
    to_core(slice(0, grouped), 0)
    for row in late_rows:
        to_core(row, row - grouped + 1)
    n_replica = CHIPS_Y * CORES * CHIPS_X
    of_row = CORES * CHIPS_X * ROWS_SENT
    received(tiles.at[0:grouped, 1 - core], core_recv.at[0])
    for row in tuple(range(grouped)) + late_rows:
        if row >= grouped:
            received(tiles.at[row, 1 - core], core_recv.at[row - grouped + 1])
        values = tiles[row].reshape(of_row, LANES).astype(jnp.int32).astype(F32)
        wide_tiles[row * of_row : (row + 1) * of_row, :] = values

    def halves(tiles_of):
        firsts, seconds = [], []
        for even, odd in zip(tiles_of[0::2], tiles_of[1::2]):
            firsts.append(jnp.where(upper, pltpu.roll(odd, GROUP, 1), even))
            seconds.append(jnp.where(upper, odd, pltpu.roll(even, GROUP, 1)))
        return jnp.concatenate([jnp.concatenate(firsts, axis=1), jnp.concatenate(seconds, axis=1)], axis=0)

    def of_all(line):
        return wide_tiles[pl.ds(line, n_replica, stride=ROWS_SENT), :]

    def across(lines, rows):
        return lax.dot_general(rows, lines.astype(BF16), (((1,), (1,)), ((), ())), preferred_element_type=F32)

    row_n = lax.broadcasted_iota(jnp.int32, (n_pairs, LANES), 0)
    lane_n = lax.broadcasted_iota(jnp.int32, (n_pairs, LANES), 1)
    of_numbers = of_all(n_pairs)
    numbers = jnp.concatenate(
        [across(of_numbers, jnp.where(lane_n == 2 * row_n + h, 1.0, 0.0).astype(BF16)) for h in range(2)], axis=1
    )
    exponents = across(of_all(n_pairs + 1), jnp.where(lane8 == 0, 1.0, 0.0).astype(BF16))[0:1, :]
    from_code = jnp.exp2(jnp.concatenate([exponents, exponents], axis=1) - TOP_BITS)
    row_place = lax.broadcasted_iota(jnp.int32, (GROUP, LANES), 0)
    place = ((row_place % BLOCK) * SIDE + row_place // BLOCK).astype(F32)
    lane64 = lax.broadcasted_iota(jnp.int32, (GROUP, LANES), 1)
    of_first = jnp.where(lane64 < GROUP, 1.0, 0.0).astype(BF16)
    of_second = jnp.where(lane64 < GROUP, 0.0, 1.0).astype(BF16)
    squares = jnp.zeros((BLOCK, LANES), F32)
    for k in range(n_pairs):
        high, low = split(of_all(k))
        where_to = jnp.where(numbers[k : k + 1, :] == place, from_code, 0.0).astype(BF16)
        both = mm(
            jnp.concatenate([where_to, where_to], axis=1),
            jnp.concatenate([high * of_first, high * of_second, low * of_first, low * of_second], axis=0),
        )
        spectra[k * GROUP : (k + 1) * GROUP, :] = both
        for q in range(SIDE):
            piece = both[q * BLOCK : (q + 1) * BLOCK, :]
            squares = squares + piece * piece
    sums_ref[0] = squares
    for other in range(SECTIONS):

        @pl.when(section != other)
        def _():
            d = (other - section + SECTIONS) % SECTIONS
            remote(sums_ref.at[0], sums_ref.at[d], SEND_Z, z_recv, (replica, other)).start()

    col_load.wait()
    tall = SIDE * GROUP
    pieces = [col_tab[i * tall : (i + 1) * tall, :] for i in range(2 * BLOCK * GROUP // LANES)]
    col_high = jnp.concatenate(pieces[: len(pieces) // 2], axis=1)
    col_low = jnp.concatenate(pieces[len(pieces) // 2 :], axis=1)
    for k in range(n_pairs):
        by_q = [spectra[k * GROUP + q * BLOCK : k * GROUP + (q + 1) * BLOCK, :] for q in range(SIDE)]
        high, low = split(halves(by_q))
        spec_high[k * 2 * BLOCK : (k + 1) * 2 * BLOCK, :] = high
        spec_low[k * 2 * BLOCK : (k + 1) * 2 * BLOCK, :] = low
    for side in range(2):
        half_cols = slice(side * 2 * LANES, (side + 1) * 2 * LANES)
        wide_cols[...] = (
            mm(spec_high[...], col_high[:, half_cols])
            + mm(spec_low[...], col_high[:, half_cols])
            + mm(spec_high[...], col_low[:, half_cols])
        )
        for k in range(n_pairs):
            by_i = []
            for a in range(2):
                lanes = slice(a * LANES, (a + 1) * LANES)
                first = wide_cols[2 * k * BLOCK : (2 * k + 1) * BLOCK, lanes]
                second = wide_cols[(2 * k + 1) * BLOCK : (2 * k + 2) * BLOCK, lanes]
                by_i.append(jnp.where(upper, pltpu.roll(second, GROUP, 1), first))
                by_i.append(jnp.where(upper, second, pltpu.roll(first, GROUP, 1)))
            high, low = split(jnp.concatenate(by_i, axis=0))
            rows = slice(side * GROUP // 2, (side + 1) * GROUP // 2)
            total_high[rows, k * LANES : (k + 1) * LANES] = high
            total_low[rows, k * LANES : (k + 1) * LANES] = low
    for s in range(OWNERS):
        cols = slice(s * width, (s + 1) * width)
        high, low = total_high[:, cols], total_low[:, cols]
        total_ref[:, cols] = mm(left_inv_ip, jnp.concatenate([high, low, high], axis=0))

    received(sums_ref.at[1:SECTIONS], z_recv)

    n_y = (CHIPS_Y - 1) * ROWS_SENT // 2
    sent(wide_tiles.at[0:n_y], SEND_Y)
    sent(tiles.at[0:3], SEND_X)
    sent(tiles.at[0:4], SEND_CORE)
    sent(sums_ref.at[1:SECTIONS], SEND_Z)


def finish(entry_count, width, nm_ref, total_ref, sums_ref, nm_out, upd_out, upd, sem):
    stores = [pltpu.make_async_copy(nm_ref, nm_out, sem.at[0])]
    stores[0].start()
    squares = jnp.sum(sums_ref[...], axis=0)
    squares = jnp.sum(jnp.sum(squares, axis=0, keepdims=True), axis=1, keepdims=True)
    scale = lax.rsqrt(squares / entry_count + epsilon)
    for k in range(OWNERS // 2):
        for s in (2 * k, 2 * k + 1):
            upd[:, s * width : (s + 1) * width] = (total_ref[:, s * width : (s + 1) * width] * scale).astype(BF16)
        cols = slice(2 * k * width, 2 * (k + 1) * width)
        stores.append(pltpu.make_async_copy(upd.at[:, cols], upd_out.at[:, cols], sem.at[1 + k]))
        stores[-1].start()
    for copy in stores:
        copy.wait()


def per_device(gradients, momentum, keep_block):
    local_rows, columns = gradients.shape[1:]
    pairs = columns // (OWNERS * LANES)
    width = pairs * LANES
    tables = jnp.asarray(constant_tables())
    col_table = jnp.asarray(column_table())
    entry_count = float(local_rows * lax.axis_size("section") * columns)
    dma = pltpu.SemaphoreType.DMA
    new_momentum, total, sums = pl.pallas_call(
        functools.partial(kernel, pairs),
        out_shape=(
            pltpu.VMEM((local_rows, columns), F32),
            pltpu.VMEM((local_rows, columns), F32),
            pltpu.VMEM((SECTIONS, BLOCK, LANES), F32),
        ),
        in_specs=[pl.BlockSpec(memory_space=pltpu.HBM)] * 5,
        out_specs=(pl.BlockSpec(memory_space=pltpu.VMEM),) * 3,
        scratch_shapes=[
            pltpu.SMEM(keep_block.shape[1:], jnp.int32),
            pltpu.VMEM(keep_block.shape[1:], jnp.int32),
            pltpu.VMEM((local_rows, columns), BF16),
            pltpu.VMEM((local_rows, columns), F32),
            pltpu.VMEM(tables.shape, BF16),
            pltpu.VMEM(col_table.shape, BF16),
            pltpu.VMEM((OWNERS * pairs * BLOCK, LANES), F32),
            pltpu.VMEM((LANES, LANES), BF16),
            pltpu.VMEM((CHIPS_Y, CORES, CHIPS_X, ROWS_SENT, LANES), jnp.int16),
            pltpu.VMEM(((CHIPS_Y * CORES * CHIPS_X + 1) * ROWS_SENT, LANES), F32),
            pltpu.VMEM((OWNERS * pairs * GROUP, LANES), F32),
            pltpu.VMEM((OWNERS * pairs * 2 * BLOCK, SIDE * GROUP), BF16),
            pltpu.VMEM((OWNERS * pairs * 2 * BLOCK, SIDE * GROUP), BF16),
            pltpu.VMEM((OWNERS * pairs * 2 * BLOCK, 2 * LANES), F32),
            pltpu.VMEM((local_rows, columns), BF16),
            pltpu.VMEM((local_rows, columns), BF16),
            dma((6,)), dma((2,)), dma((4,)), dma((CHIPS_Y,)), dma((5,)), dma((5,)), dma,
        ],
        compiler_params=pltpu.CompilerParams(collective_id=0, has_side_effects=True, vmem_limit_bytes=56 << 20),
        name="kept_blocks_step",
    )(keep_block[0], gradients[0], momentum[0], tables, col_table)
    hbm = pl.BlockSpec(memory_space=pltpu.HBM)
    new_momentum, update = pl.pallas_call(
        functools.partial(finish, entry_count, width),
        out_shape=(
            jax.ShapeDtypeStruct((local_rows, columns), F32),
            jax.ShapeDtypeStruct((local_rows, columns), BF16),
        ),
        in_specs=[pl.BlockSpec(memory_space=pltpu.VMEM)] * 3,
        out_specs=(hbm, hbm),
        scratch_shapes=[pltpu.VMEM((local_rows, columns), BF16), dma((1 + OWNERS // 2,))],
        compiler_params=pltpu.CompilerParams(vmem_limit_bytes=32 << 20),
        name="scale_and_store",
    )(new_momentum, total, sums)
    return new_momentum[None], update


def solution(mesh):
    placed = (
        P("replica", "section", None),
        P("replica", "section", None),
        P("replica", "section", None),
    )
    return jax.shard_map(
        per_device,
        mesh=mesh,
        in_specs=placed,
        out_specs=(P("replica", "section", None), P("section", None)),
        check_vma=False,
    )
```
